512 devices in a mesh: dp: 32 (over z_hi, y, core), ctx: 4 (over z_lo), rep: 4 (over x).
Axes of the slice: x: 4, y: 8, z: 8 (z_hi: 2, z_lo: 4; z = z_hi * 4 + z_lo), core: 2. Of those that a mesh axis runs over, the one named last changes fastest.
Arguments:
- tokens: bfloat16 [32768, 4096], P(('dp', 'rep'), 'ctx'), may hold values from -6 to 6
- cotangent: bfloat16 [32768, 4096], P(('dp', 'rep'), 'ctx'), may hold values from -6 to 6
- routes: int32 [32768, 8], P(('dp', 'rep')), may hold values from 0 to 127, all different within a row
- gates: float32 [32768, 8], P(('dp', 'rep')), may hold values from 0.05 to 0.6
- replica_of: int32 [2048], P(('dp', 'rep')), may hold values from 0 to 3
- capacity: int32 [32], replicated, may hold values from 1 to 2, as said below
- w_gate: bfloat16 [32, 4096, 768], P('dp', ('ctx', 'rep')), may hold values from -0.09375 to 0.09375
- w_up: bfloat16 [32, 4096, 768], P('dp', ('ctx', 'rep')), may hold values from -0.09375 to 0.09375
- w_down: bfloat16 [32, 768, 4096], P('dp', None, ('ctx', 'rep')), may hold values from -0.21875 to 0.21875
Outputs:
- layer_out: bfloat16 [32768, 4096], P(('dp', 'rep'), 'ctx')
- input_grad: bfloat16 [32768, 4096], P(('dp', 'rep'), 'ctx')
- grad_gate: bfloat16 [32, 4096, 768], P('dp', ('ctx', 'rep'))
- grad_up: bfloat16 [32, 4096, 768], P('dp', ('ctx', 'rep'))
- grad_down: bfloat16 [32, 768, 4096], P('dp', None, ('ctx', 'rep'))
The draws below stay inside these ranges and needn't reach their ends.
Inputs may be any that keep to these rules, and one draw needn't show every extreme that they name: Some expert has capacity exactly 2.
All inputs are finite; a program needn't handle non-finite values.
Results may differ from the reference program's by a relative error of at most 0.029.
Values may be sent and summed in bfloat16 or wider, within the bound.
A program may use at most 128 MiB of HBM per device.

```python
import jax
import jax.numpy as jnp
from jax import lax

D = 4096
HID = 768
TOP = 8
BLK = 16
TOK_G = 256
FLIGHT = 32
EXPERTS = 128
CAP = 2
TOKENS = 32768
N_DP = 32
N_REP = 4


def draw_capacity(key, part):
    key = jax.random.fold_in(key, 11)
    first_key, second_key = jax.random.split(key)
    values = jax.random.randint(first_key, (FLIGHT,), 1, CAP + 1)
    chosen = jax.random.randint(second_key, (), 0, FLIGHT)
    return jnp.where(jnp.arange(FLIGHT) == chosen, CAP, values).astype(jnp.int32)


def place_ends(array, stream_key, low, high):
    longest = array.shape.index(max(array.shape))
    spots = []
    for shift in (0, 1):
        where = [jax.random.randint(jax.random.fold_in(stream_key, axis), (), 0, length) for axis, length in enumerate(array.shape)]
        where[longest] = (where[longest] + shift) % array.shape[longest]
        spots.append(tuple(where))
    return array.at[spots[0]].set(low).at[spots[1]].set(high)


def steps_of(rng, shape, cuts, least, high):
    def one(position, shards_of):
        heights = jax.random.uniform(jax.random.fold_in(jax.random.fold_in(rng, 6), position), (shards_of,), jnp.float32, least / len(cuts), high / len(cuts))
        return jnp.repeat(jnp.exp(heights), shape[position] // shards_of).reshape((-1,) + (1,) * (len(shape) - position - 1))

    gain = one(*cuts[0])
    for cut in cuts[1:]:
        gain = gain * one(*cut)
    return gain


def distinct(key, rows, count, top, lift):
    order = jax.random.permutation(jax.random.fold_in(key, 1), count)
    boost = order
    for power in range(3):
        boost = boost * boost // count
    boost = boost * lift // count
    tickets = jax.random.randint(jax.random.fold_in(key, 2), (rows, count), 0, 4096) + boost
    holders = jax.random.permutation(jax.random.fold_in(key, 3), rows)[jnp.arange(count) % rows]
    tickets = jnp.where(jnp.arange(rows)[:, None] == holders[None, :], 1 << 14, tickets)
    priority = tickets * count + jnp.arange(count)
    return lax.top_k(priority.astype(jnp.int32), top)[1].astype(jnp.int32)


def centred(own_key, shape, spread, limit, pieces=(), kind=jnp.bfloat16):
    loudness = steps_of(own_key, shape, pieces, -0.22, 0.18) if pieces else 1.0
    array = jax.random.normal(own_key, shape, jnp.float32) * spread * loudness
    return jnp.minimum(jnp.maximum(array, -limit), limit).astype(kind)


def setup_inputs(seed: int = 0) -> dict:
    seeds = jax.random.split(jax.random.key(seed), 10)
    tokens = centred(seeds[0], (TOKENS, D), 1.0, 6.0, ((0, 128), (1, 4)))
    cotangent = centred(seeds[1], (TOKENS, D), 1.0, 6.0, ((0, 128), (1, 4)))
    routes = distinct(seeds[2], TOKENS, EXPERTS, TOP, 1024)
    gates = jnp.clip(0.05 + 0.55 * jax.random.uniform(seeds[3], (TOKENS, TOP), jnp.float32) ** steps_of(seeds[3], (TOKENS, TOP), ((0, 128),), -0.2, 0.2), 0.05, 0.6)
    replica_of = place_ends(jax.random.randint(seeds[4], (TOKENS // BLK,), 0, N_REP), jax.random.fold_in(seeds[4], 1), 0, N_REP - 1).astype(jnp.int32)
    capacity = draw_capacity(jax.random.fold_in(seeds[9], 71), 0)
    w_gate = centred(seeds[6], (FLIGHT, D, HID), D ** -0.5, 0.09375, ((0, 32), (1, 16)))
    w_up = centred(seeds[7], (FLIGHT, D, HID), D ** -0.5, 0.09375, ((0, 32), (1, 16)))
    w_down = centred(seeds[8], (FLIGHT, HID, D), HID ** -0.5, 0.21875, ((0, 32), (2, 16)))
    return {"tokens": tokens, "cotangent": cotangent, "routes": routes, "gates": gates, "replica_of": replica_of, "capacity": capacity, "w_gate": w_gate, "w_up": w_up, "w_down": w_down}


def route_slots(routes, replica_of, capacity, expert_total, replica_count, slot_count, block_size):
    token_count = routes.shape[0]
    replica = jnp.broadcast_to(replica_of[:, None], (replica_of.shape[0], block_size)).reshape(token_count)
    pending_transfers = routes < expert_total
    bucket = routes * replica_count + replica[:, None]
    limits = jnp.sum(jnp.where(routes[:, :, None] == jnp.arange(expert_total, dtype=jnp.int32), capacity, 0), axis=2)
    flat_bucket = bucket.T.reshape(-1)
    flattened_live_rows = pending_transfers.T.reshape(-1)
    onehot = ((flat_bucket[:, None] == jnp.arange(expert_total * replica_count, dtype=jnp.int32)[None, :]) & flattened_live_rows[:, None]).astype(jnp.int32)
    before = jnp.cumsum(onehot, axis=0) - onehot
    slots = jnp.sum(before * onehot, axis=1).astype(jnp.int32)
    retained = flattened_live_rows & (slots < limits.T.reshape(-1))
    return flat_bucket, slots, retained


def activations(pre_gate, pre_up, back):
    sigmoid_gate = jax.nn.sigmoid(pre_gate)
    swish_gate = pre_gate * sigmoid_gate
    hidden_activation = (swish_gate * pre_up).astype(jnp.bfloat16)
    d_gate = (back * pre_up * sigmoid_gate * (1.0 + pre_gate * (1.0 - sigmoid_gate))).astype(jnp.bfloat16)
    d_up = (back * swish_gate).astype(jnp.bfloat16)
    return hidden_activation, d_gate, d_up


def reference(tokens, cotangent, routes, gates, replica_of, capacity, w_gate, w_up, w_down):
    groups = N_DP * N_REP
    mapped = jax.vmap(route_slots, in_axes=(0, 0, None, None, None, None, None))
    buckets, slots, retained = mapped(routes.reshape(groups, TOK_G, TOP), replica_of.reshape(groups, TOK_G // BLK), capacity, N_DP, N_REP, CAP, BLK)

    def token_order(values):
        return jnp.transpose(values.reshape(groups, TOP, TOK_G), (0, 2, 1)).reshape(TOKENS, TOP)

    buckets = token_order(buckets)
    slots = token_order(slots)
    retained = token_order(retained)
    expert_of = buckets // N_REP
    replica = buckets % N_REP
    group_index = (jnp.arange(TOKENS, dtype=jnp.int32) // TOK_G)[:, None]
    place = ((replica * groups + group_index) * CAP + slots).astype(jnp.int32)
    total_rows = N_REP * groups * CAP

    def per_expert(carry, inputs):
        out_acc, grad_acc = carry
        expert, weight_gate, weight_up, weight_down = inputs
        match = retained & (expert_of == expert)
        present = jnp.any(match, axis=1)
        target = jnp.where(present, jnp.sum(jnp.where(match, place, 0), axis=1), total_rows).astype(jnp.int32)
        gate_here = jnp.sum(jnp.where(match, gates, 0.0), axis=1)
        rows_in = jnp.zeros((total_rows, D), jnp.bfloat16).at[target].set(tokens, mode="drop")
        grads_in = jnp.zeros((total_rows, D), jnp.bfloat16).at[target].set(cotangent, mode="drop")
        gate_in = jnp.zeros((total_rows,), jnp.float32).at[target].set(gate_here, mode="drop")
        scaled = (gate_in[:, None] * grads_in).astype(jnp.bfloat16)
        pre_gate = jnp.dot(rows_in, weight_gate, preferred_element_type=jnp.float32)
        pre_up = jnp.dot(rows_in, weight_up, preferred_element_type=jnp.float32)
        back = jnp.dot(scaled, weight_down.T, preferred_element_type=jnp.float32)
        hidden_activation, d_gate, d_up = activations(pre_gate, pre_up, back)
        contribution = (gate_in[:, None] * jnp.dot(hidden_activation, weight_down, preferred_element_type=jnp.float32)).astype(jnp.bfloat16)
        row_grad = (jnp.dot(d_gate, weight_gate.T, preferred_element_type=jnp.float32) + jnp.dot(d_up, weight_up.T, preferred_element_type=jnp.float32)).astype(jnp.bfloat16)
        rows_q = rows_in.reshape(N_REP, groups * CAP, D).astype(jnp.float32)
        scaled_q = scaled.reshape(N_REP, groups * CAP, D).astype(jnp.float32)
        hidden_q = hidden_activation.reshape(N_REP, groups * CAP, HID).astype(jnp.float32)
        part_gate = jnp.einsum("qrd,qrh->qdh", rows_q, d_gate.reshape(N_REP, groups * CAP, HID).astype(jnp.float32)).astype(jnp.bfloat16)
        partial_up_projection = jnp.einsum("qrd,qrh->qdh", rows_q, d_up.reshape(N_REP, groups * CAP, HID).astype(jnp.float32)).astype(jnp.bfloat16)
        part_down = jnp.einsum("qrh,qrd->qhd", hidden_q, scaled_q).astype(jnp.bfloat16)
        grad_gate = jnp.sum(part_gate.astype(jnp.float32), axis=0).astype(jnp.bfloat16)
        grad_up = jnp.sum(partial_up_projection.astype(jnp.float32), axis=0).astype(jnp.bfloat16)
        grad_down = jnp.sum(part_down.astype(jnp.float32), axis=0).astype(jnp.bfloat16)
        safe = jnp.minimum(target, total_rows - 1)
        picked_out = jnp.take(contribution, safe, axis=0).astype(jnp.float32)
        picked_grad = jnp.take(row_grad, safe, axis=0).astype(jnp.float32)
        out_acc = out_acc + jnp.where(present[:, None], picked_out, 0.0)
        grad_acc = grad_acc + jnp.where(present[:, None], picked_grad, 0.0)
        return (out_acc, grad_acc), (grad_gate, grad_up, grad_down)

    start = (jnp.zeros((TOKENS, D), jnp.float32), jnp.zeros((TOKENS, D), jnp.float32))
    inputs = (jnp.arange(FLIGHT, dtype=jnp.int32), w_gate, w_up, w_down)
    (out_acc, grad_acc), (grad_gate, grad_up, grad_down) = lax.scan(per_expert, start, inputs)
    return out_acc.astype(jnp.bfloat16), grad_acc.astype(jnp.bfloat16), grad_gate, grad_up, grad_down
```

```python
import functools

import jax
import jax.numpy as jnp
from jax import lax
from jax.experimental import pallas as pl
from jax.experimental.pallas import tpu as pltpu
from jax.sharding import PartitionSpec as P

MESH = pl.DeviceIdType.MESH
BF = jnp.bfloat16
F32 = jnp.float32
BLK = 16
CAP = 2
LANES = 128
HID_CHUNKS = 3
VMEM_BYTES = 58 * 1024 * 1024


def dot(left, right):
    return jnp.dot(left, right, preferred_element_type=F32)


def dot_first(left, right):
    return lax.dot_general(left, right, (((0,), (0,)), ((), ())), preferred_element_type=F32)


def dot_last(left, right):
    return lax.dot_general(left, right, (((1,), (1,)), ((), ())), preferred_element_type=F32)


def pack(stage, array, slot, rows, buckets, tiles):
    lines = 2 * CAP * tiles
    for tile in range(tiles):
        first = (array * CAP + slot) * tiles + tile
        stage[pl.ds(first, buckets, stride=lines), :] = rows[:, tile * LANES : (tile + 1) * LANES]


def unpack(stage, array, slot, tile, buckets, tiles):
    lines = 2 * CAP * tiles
    first = (array * CAP + slot) * tiles + tile
    return stage[pl.ds(first, buckets, stride=lines), :]


def dispatch_kernel(
    n_dp, n_rep, replica, capacity, routes, gates, tokens, cotangent, send, pick, pick_hi, pick_lo, stage
):
    count, top = routes.shape
    buckets = n_dp * n_rep
    tiles = tokens.shape[1] // LANES
    token = lax.broadcasted_iota(jnp.int32, (count, 1), 0)
    serve = jnp.zeros((count, 1), jnp.int32)
    for block in range(count // BLK):
        serve = jnp.where(token // BLK == block, replica[block], serve)
    lane = lax.broadcasted_iota(jnp.int32, (1, buckets), 1)
    limit = jnp.zeros((1, buckets), jnp.int32)
    for expert in range(n_dp):
        limit = jnp.where(lane // n_rep == expert, capacity[expert], limit)
    limit = limit.astype(F32)
    lanes = lax.broadcasted_iota(jnp.int32, (count, buckets), 1)
    earlier = (
        lax.broadcasted_iota(jnp.int32, (count, count), 0)
        > lax.broadcasted_iota(jnp.int32, (count, count), 1)
    ).astype(F32).astype(BF)
    total = jnp.zeros((1, buckets), F32)
    kept = [jnp.zeros((count, buckets), F32) for _ in range(CAP)]
    weight = [jnp.zeros((count, buckets), F32) for _ in range(CAP)]
    for k in range(top):
        hit = lanes == routes[:, k : k + 1] * n_rep + serve
        ones = jnp.where(hit, 1.0, 0.0)
        slot_of = dot(earlier, ones.astype(BF)) + total
        total = total + jnp.sum(ones, axis=0, keepdims=True)
        gate = gates[:, k : k + 1]
        for slot in range(CAP):
            here = jnp.where((slot_of == float(slot)) & (limit > float(slot)), ones, 0.0)
            kept[slot] = kept[slot] + here
            weight[slot] = weight[slot] + here * gate
    rows = tokens[...]
    grads = cotangent[...]
    for slot in range(CAP):
        columns = slice(slot * buckets, (slot + 1) * buckets)
        chosen = kept[slot].astype(BF)
        high = weight[slot].astype(BF)
        low = (weight[slot] - high.astype(F32)).astype(BF)
        pick[:, columns] = chosen
        pick_hi[:, columns] = high
        pick_lo[:, columns] = low
        pack(stage, 0, slot, dot_first(chosen, rows), buckets, tiles)
        pack(stage, 1, slot, dot_first(high, grads) + dot_first(low, grads), buckets, tiles)
    send[...] = stage[...].astype(BF).reshape(send.shape)


def combine_kernel(back, pick, pick_hi, pick_lo, layer_out, input_grad, stage):
    buckets = back.shape[0]
    tiles = layer_out.shape[1] // LANES
    stage[...] = back[...].astype(F32).reshape(stage.shape)
    for array in range(2):
        for tile in range(tiles):
            rows = jnp.concatenate(
                [unpack(stage, array, slot, tile, buckets, tiles) for slot in range(CAP)], axis=0
            ).astype(BF)
            columns = slice(tile * LANES, (tile + 1) * LANES)
            if array == 0:
                layer_out[:, columns] = (dot(pick_hi[...], rows) + dot(pick_lo[...], rows)).astype(BF)
            else:
                input_grad[:, columns] = dot(pick[...], rows).astype(BF)


def expert_kernel(
    n_dp,
    n_ctx,
    n_rep,
    send,
    w_gate,
    w_up,
    w_down,
    back,
    grad_gate,
    grad_up,
    grad_down,
    arrived,
    all_gate,
    all_up,
    all_down,
    stage,
    rows,
    scaled,
    part,
    part_in,
    act,
    total_out,
    total_grad,
    back_send,
    grad_part,
    grad_in,
    local_sem,
    row_sem,
    weight_send,
    weight_recv,
    part_sem,
    act_sem,
    back_sem,
    grad_sem,
):
    buckets = n_dp * n_rep
    my_dp, my_ctx, my_rep = (lax.axis_index(name) for name in ("dp", "ctx", "rep"))
    me = my_dp * n_rep + my_rep
    width = rows.shape[1]
    tiles = width // LANES
    piece = width // n_rep
    chunk = act.shape[3]
    chunks = act.shape[0]
    row_count = rows.shape[0]
    share = row_count // n_ctx
    mine = pl.ds(pl.multiple_of(my_ctx * share, share), share)

    def hid(h):
        return pl.ds(h * chunk, chunk)

    def weight_views(h):
        return (
            (w_gate.at[:, hid(h)], lambda q: all_gate.at[q, :, hid(h)]),
            (w_up.at[:, hid(h)], lambda q: all_up.at[q, :, hid(h)]),
            (w_down.at[hid(h), :], lambda q: all_down.at[q, hid(h), :]),
        )

    def send_weights(h):
        for kind, (source, target) in enumerate(weight_views(h)):
            for step in range(1, n_rep):
                pltpu.make_async_remote_copy(
                    src_ref=source,
                    dst_ref=target(my_rep),
                    send_sem=weight_send.at[h, kind],
                    recv_sem=weight_recv.at[h, kind],
                    device_id={"rep": lax.rem(my_rep + step, n_rep)},
                    device_id_type=MESH,
                ).start()

    def wait_weights(h, sem):
        for kind, wide in enumerate(
            (
                all_gate.at[pl.ds(0, n_rep - 1), :, hid(h)],
                all_up.at[pl.ds(0, n_rep - 1), :, hid(h)],
                all_down.at[pl.ds(0, n_rep - 1), hid(h), :],
            )
        ):
            pltpu.make_async_copy(wide, wide, sem.at[h, kind]).wait()

    own = [
        pltpu.make_async_copy(w_gate, all_gate.at[my_rep], local_sem.at[0]),
        pltpu.make_async_copy(w_up, all_up.at[my_rep], local_sem.at[1]),
        pltpu.make_async_copy(w_down, all_down.at[my_rep], local_sem.at[2]),
    ]
    for copy in own:
        copy.start()

    def exchange(source, target, sem):
        def one(step, carry):
            other = lax.rem(me + step, buckets)
            pltpu.make_async_remote_copy(
                src_ref=source.at[other],
                dst_ref=target.at[me],
                send_sem=sem.at[0],
                recv_sem=sem.at[1],
                device_id={"dp": other // n_rep, "rep": lax.rem(other, n_rep)},
                device_id_type=MESH,
            ).start()
            return carry

        lax.fori_loop(1, buckets, one, 0)
        target[me] = source[me]

    def wait_exchange(target, sem):
        rest = target.at[pl.ds(0, buckets - 1)]
        pltpu.make_async_copy(rest, rest, sem).wait()

    exchange(send, arrived, row_sem)
    for h in range(chunks):
        send_weights(h)
    for copy in own:
        copy.wait()
    wait_exchange(arrived, row_sem.at[1])
    stage[...] = arrived[...].astype(F32).reshape(stage.shape)
    for array, target in enumerate((rows, scaled)):
        for slot in range(CAP):
            for tile in range(tiles):
                target[slot * buckets : (slot + 1) * buckets, tile * LANES : (tile + 1) * LANES] = unpack(
                    stage, array, slot, tile, buckets, tiles
                ).astype(BF)

    def send_part(h):
        wait_weights(h, weight_recv)
        for kind, full in enumerate((all_gate, all_up)):
            block = full[:, :, h * chunk : (h + 1) * chunk].reshape(width, chunk)
            part[h, kind] = dot(rows[...], block).astype(BF)
        sums = None
        for q in range(n_rep):
            term = dot_last(
                scaled[:, q * piece : (q + 1) * piece], all_down[q, h * chunk : (h + 1) * chunk, :]
            )
            sums = term if sums is None else sums + term
        part[h, 2] = sums.astype(BF)
        for step in range(1, n_ctx):
            other = lax.rem(my_ctx + step, n_ctx)
            pltpu.make_async_remote_copy(
                src_ref=part.at[h, :, pl.ds(pl.multiple_of(other * share, share), share), :],
                dst_ref=part_in.at[h, my_ctx],
                send_sem=part_sem.at[h, 0],
                recv_sem=part_sem.at[h, 1],
                device_id={"ctx": other},
                device_id_type=MESH,
            ).start()
        part_in[h, my_ctx] = part[h, :, mine, :]

    def wait_part(h, side):
        rest = part_in.at[h, pl.ds(0, n_ctx - 1)]
        pltpu.make_async_copy(rest, rest, part_sem.at[h, side]).wait()

    def send_act(h):
        wait_part(h, 1)
        pre_gate, pre_up, grad = (
            sum(part_in[h, c, kind].astype(F32) for c in range(n_ctx)) for kind in range(3)
        )
        sigmoid = jax.nn.sigmoid(pre_gate)
        swish = pre_gate * sigmoid
        act[h, 0, mine, :] = (swish * pre_up).astype(BF)
        act[h, 1, mine, :] = (grad * pre_up * sigmoid * (1.0 + pre_gate * (1.0 - sigmoid))).astype(BF)
        act[h, 2, mine, :] = (grad * swish).astype(BF)
        for step in range(1, n_ctx):
            block = act.at[h, :, mine, :]
            pltpu.make_async_remote_copy(
                src_ref=block,
                dst_ref=block,
                send_sem=act_sem.at[h, 0],
                recv_sem=act_sem.at[h, 1],
                device_id={"ctx": lax.rem(my_ctx + step, n_ctx)},
                device_id_type=MESH,
            ).start()

    def wait_act(h, side):
        rest = act.at[h, :, pl.ds(0, (n_ctx - 1) * share), :]
        pltpu.make_async_copy(rest, rest, act_sem.at[h, side]).wait()

    def add_outputs(h):
        wait_act(h, 1)
        for q in range(n_rep):
            columns = slice(q * piece, (q + 1) * piece)
            out = dot(act[h, 0], all_down[q, h * chunk : (h + 1) * chunk, :])
            grad = dot_last(act[h, 1], all_gate[q, :, h * chunk : (h + 1) * chunk]) + dot_last(
                act[h, 2], all_up[q, :, h * chunk : (h + 1) * chunk]
            )
            if h:
                out = out + total_out[:, columns]
                grad = grad + total_grad[:, columns]
            total_out[:, columns] = out
            total_grad[:, columns] = grad

    def send_outputs():
        for slot in range(CAP):
            taken = slice(slot * buckets, (slot + 1) * buckets)
            pack(stage, 0, slot, total_out[taken, :], buckets, tiles)
            pack(stage, 1, slot, total_grad[taken, :], buckets, tiles)
        back_send[...] = stage[...].astype(BF).reshape(back_send.shape)
        exchange(back_send, back, back_sem)

    def send_grads(h):
        for q in range(n_rep):
            columns = slice(q * piece, (q + 1) * piece)
            grad_part[h, q, 0] = dot_first(rows[:, columns], act[h, 1]).astype(BF)
            grad_part[h, q, 1] = dot_first(rows[:, columns], act[h, 2]).astype(BF)
            grad_part[h, q, 2] = dot_first(act[h, 0], scaled[:, columns]).astype(BF)
        for step in range(1, n_rep):
            other = lax.rem(my_rep + step, n_rep)
            pltpu.make_async_remote_copy(
                src_ref=grad_part.at[h, other],
                dst_ref=grad_in.at[h, my_rep],
                send_sem=grad_sem.at[h, 0],
                recv_sem=grad_sem.at[h, 1],
                device_id={"rep": other},
                device_id_type=MESH,
            ).start()
        grad_in[h, my_rep] = grad_part[h, my_rep]

    def wait_grads(h, side):
        rest = grad_in.at[h, pl.ds(0, n_rep - 1)]
        pltpu.make_async_copy(rest, rest, grad_sem.at[h, side]).wait()

    def add_grads(h):
        wait_grads(h, 1)
        sums = [sum(grad_in[h, q, kind].astype(F32) for q in range(n_rep)).astype(BF) for kind in range(3)]
        grad_gate[:, h * chunk : (h + 1) * chunk] = sums[0]
        grad_up[:, h * chunk : (h + 1) * chunk] = sums[1]
        grad_down[h * chunk : (h + 1) * chunk, :] = sums[2]

    send_part(0)
    for h in range(1, chunks):
        send_part(h)
        send_act(h - 1)
    if chunks > 1:
        add_outputs(0)
        send_grads(0)
    send_act(chunks - 1)
    for h in range(1, chunks - 1):
        add_outputs(h)
        send_grads(h)
    add_outputs(chunks - 1)
    send_outputs()
    send_grads(chunks - 1)
    wait_exchange(back, back_sem.at[1])
    for h in range(chunks):
        add_grads(h)
    wait_exchange(arrived, row_sem.at[0])
    wait_exchange(back, back_sem.at[0])
    for h in range(chunks):
        wait_weights(h, weight_send)
        wait_part(h, 0)
        wait_act(h, 0)
        wait_grads(h, 0)


def per_device(n_dp, n_ctx, n_rep, tokens, cotangent, routes, gates, replica_of, capacity, w_gate, w_up, w_down):
    count, width = tokens.shape
    buckets = n_dp * n_rep
    slots = CAP * buckets
    tiles = width // LANES
    lines = 2 * CAP * tiles
    piece = width // n_rep
    hidden = w_gate.shape[2]
    chunk = hidden // HID_CHUNKS
    share = slots // n_ctx
    vmem = pl.BlockSpec(memory_space=pltpu.VMEM)
    smem = pl.BlockSpec(memory_space=pltpu.SMEM)
    hbm = pl.BlockSpec(memory_space=pl.ANY)
    params = functools.partial(pltpu.CompilerParams, vmem_limit_bytes=VMEM_BYTES)
    message = jax.ShapeDtypeStruct((buckets, lines, LANES), BF)
    matrix = jax.ShapeDtypeStruct((count, slots), BF)
    stage = pltpu.VMEM((buckets * lines, LANES), F32)
    send, pick, pick_hi, pick_lo = pl.pallas_call(
        functools.partial(dispatch_kernel, n_dp, n_rep),
        out_shape=(message, matrix, matrix, matrix),
        in_specs=[smem, smem, vmem, vmem, vmem, vmem],
        out_specs=[vmem] * 4,
        scratch_shapes=[stage],
        compiler_params=params(),
        name="dispatch",
    )(replica_of, capacity, routes, gates, tokens, cotangent)
    chunks = HID_CHUNKS
    back, grad_gate, grad_up, grad_down = pl.pallas_call(
        functools.partial(expert_kernel, n_dp, n_ctx, n_rep),
        out_shape=(
            message,
            jax.ShapeDtypeStruct((piece, hidden), BF),
            jax.ShapeDtypeStruct((piece, hidden), BF),
            jax.ShapeDtypeStruct((hidden, piece), BF),
        ),
        in_specs=[vmem, hbm, hbm, hbm],
        out_specs=[vmem] * 4,
        scratch_shapes=[
            pltpu.VMEM((buckets, lines, LANES), BF),
            pltpu.VMEM((n_rep, piece, hidden), BF),
            pltpu.VMEM((n_rep, piece, hidden), BF),
            pltpu.VMEM((n_rep, hidden, piece), BF),
            stage,
            pltpu.VMEM((slots, width), BF),
            pltpu.VMEM((slots, width), BF),
            pltpu.VMEM((chunks, 3, slots, chunk), BF),
            pltpu.VMEM((chunks, n_ctx, 3, share, chunk), BF),
            pltpu.VMEM((chunks, 3, slots, chunk), BF),
            pltpu.VMEM((slots, width), F32),
            pltpu.VMEM((slots, width), F32),
            pltpu.VMEM((buckets, lines, LANES), BF),
            pltpu.VMEM((chunks, n_rep, 3, piece, chunk), BF),
            pltpu.VMEM((chunks, n_rep, 3, piece, chunk), BF),
            pltpu.SemaphoreType.DMA((3,)),
            pltpu.SemaphoreType.DMA((2,)),
            pltpu.SemaphoreType.DMA((chunks, 3)),
            pltpu.SemaphoreType.DMA((chunks, 3)),
            pltpu.SemaphoreType.DMA((chunks, 2)),
            pltpu.SemaphoreType.DMA((chunks, 2)),
            pltpu.SemaphoreType.DMA((2,)),
            pltpu.SemaphoreType.DMA((chunks, 2)),
        ],
        compiler_params=params(has_side_effects=True),
        name="experts",
    )(send, w_gate[0], w_up[0], w_down[0])
    layer_out, input_grad = pl.pallas_call(
        combine_kernel,
        out_shape=(jax.ShapeDtypeStruct((count, width), BF),) * 2,
        in_specs=[vmem] * 4,
        out_specs=[vmem] * 2,
        scratch_shapes=[stage],
        compiler_params=params(),
        name="combine",
    )(back, pick, pick_hi, pick_lo)
    return layer_out, input_grad, grad_gate[None], grad_up[None], grad_down[None]


def solution(mesh):
    rows = P(("dp", "rep"), "ctx")
    routed = P(("dp", "rep"), None)
    tall = P("dp", ("ctx", "rep"), None)
    wide = P("dp", None, ("ctx", "rep"))
    sizes = dict(mesh.shape)
    return jax.shard_map(
        functools.partial(per_device, sizes["dp"], sizes["ctx"], sizes["rep"]),
        mesh=mesh,
        in_specs=(rows, rows, routed, routed, P(("dp", "rep")), P(), tall, tall, wide),
        out_specs=(rows, rows, tall, tall, wide),
        check_vma=False,
    )
```

```python
import functools

import jax
import jax.numpy as jnp
from jax import lax
from jax.experimental import pallas as pl
from jax.experimental.pallas import tpu as pltpu
from jax.sharding import PartitionSpec as P

MESH = pl.DeviceIdType.MESH
BF = jnp.bfloat16
F32 = jnp.float32
BLK = 16
CAP = 2
LANES = 128
HID_CHUNKS = (384, 256, 128)
VMEM_BYTES = 58 * 1024 * 1024


def dot(left, right):
    return jnp.dot(left, right, preferred_element_type=F32)


def dot_first(left, right):
    return lax.dot_general(left, right, (((0,), (0,)), ((), ())), preferred_element_type=F32)


def dot_last(left, right):
    return lax.dot_general(left, right, (((1,), (1,)), ((), ())), preferred_element_type=F32)


def pack(stage, slot, rows, buckets, tiles):
    for tile in range(tiles):
        stage[pl.ds(slot * tiles + tile, buckets, stride=CAP * tiles), :] = rows[:, tile * LANES : (tile + 1) * LANES]


def unpack(stage, slot, tile, buckets, tiles):
    return stage[pl.ds(slot * tiles + tile, buckets, stride=CAP * tiles), :]


def expert_kernel(
    n_dp,
    n_ctx,
    n_rep,
    replica,
    capacity,
    routes,
    gates,
    tokens,
    cotangent,
    w_gate,
    w_up,
    w_down,
    layer_out,
    input_grad,
    grad_gate,
    grad_up,
    grad_down,
    token_rows,
    cotangent_rows,
    pick,
    pick_hi,
    pick_lo,
    leave,
    arrive,
    back_leave,
    back_arrive,
    all_gate,
    all_up,
    all_down,
    stage,
    rows,
    part,
    inbox,
    cross,
    act,
    total,
    grad_part,
    grad_relay,
    grad_in,
    out_rows,
    out_tall,
    out_wide,
    local_sem,
    row_sem,
    weight_sem,
    part_sem,
    act_sem,
    back_sem,
    relay_sem,
    grad_sem,
    out_sem,
):
    buckets = n_dp * n_rep
    my_dp, my_ctx, my_rep = (lax.axis_index(name) for name in ("dp", "ctx", "rep"))
    me = my_dp * n_rep + my_rep
    right, left = lax.rem(my_rep + 1, n_rep), lax.rem(my_rep + n_rep - 1, n_rep)
    beside = (right, left)
    across = lax.rem(my_rep + 2, n_rep)
    count, width = tokens.shape
    top = routes.shape[0]
    tiles = width // LANES
    piece = width // n_rep
    chunks = len(HID_CHUNKS)
    ends = [sum(HID_CHUNKS[: h + 1]) for h in range(chunks)]
    hid = [slice(end - size, end) for end, size in zip(ends, HID_CHUNKS)]
    share = rows.shape[1] // 2
    inner = jnp.logical_or(my_ctx == 1, my_ctx == 2)
    outer = jnp.logical_not(inner)
    partner = my_ctx + 1 - 2 * lax.rem(my_ctx, 2)
    opposite = n_ctx - 1 - my_ctx
    mine = pl.ds(pl.multiple_of((my_ctx // 2) * share, share), share)
    theirs = pl.ds(pl.multiple_of((1 - my_ctx // 2) * share, share), share)
    groups = (slice(0, 2), slice(2, 3))
    act_groups = (slice(0, 1), slice(1, 3))
    halves = (slice(0, piece // 2), slice(piece // 2, piece))

    def remote(source, target, sem, where):
        return pltpu.make_async_remote_copy(
            src_ref=source,
            dst_ref=target,
            send_sem=sem[0],
            recv_sem=sem[1],
            device_id=where,
            device_id_type=MESH,
        )

    def wait_for(view, sem):
        pltpu.make_async_copy(view, view, sem).wait()

    barrier = pltpu.get_barrier_semaphore()

    reps = [lax.rem(my_rep + step, n_rep) for step in range(n_rep)]

    def to_others(visit):
        def one(step, carry):
            other = lax.rem(my_dp + step, n_dp)
            for rep in reps:
                visit(other, rep)
            return carry

        lax.fori_loop(1, n_dp, one, 0)
        for rep in reps[1:]:
            visit(my_dp, rep)

    def greet(dp, rep):
        pl.semaphore_signal(barrier, inc=1, device_id={"dp": dp, "rep": rep}, device_id_type=MESH)

    with jax.named_scope("greet"):
        to_others(greet)
        for step in range(1, n_ctx):
            pl.semaphore_signal(
                barrier, inc=1, device_id={"ctx": lax.rem(my_ctx + step, n_ctx)}, device_id_type=MESH
            )
        loads = [
            pltpu.make_async_copy(source, target, local_sem.at[kind])
            for kind, (source, target) in enumerate(
                (
                    (tokens, token_rows),
                    (cotangent, cotangent_rows),
                    (w_gate, all_gate.at[my_rep]),
                    (w_up, all_up.at[my_rep]),
                    (w_down, all_down.at[my_rep]),
                )
            )
        ]
        for copy in loads:
            copy.start()

    with jax.named_scope("slots"):
        token = lax.broadcasted_iota(jnp.int32, (1, count), 1)
        serve = jnp.zeros((1, count), jnp.int32)
        for block in range(count // BLK):
            serve = jnp.where(token // BLK == block, replica[block], serve)
        bucket = lax.broadcasted_iota(jnp.int32, (buckets, 1), 0)
        limit = jnp.zeros((buckets, 1), jnp.int32)
        for expert in range(n_dp):
            limit = jnp.where(bucket // n_rep == expert, capacity[expert], limit)
        limit = limit.astype(F32)
        bucket = lax.broadcasted_iota(jnp.int32, (buckets, count), 0)
        earlier = jnp.where(
            lax.broadcasted_iota(jnp.int32, (count, count), 0) < lax.broadcasted_iota(jnp.int32, (count, count), 1),
            1.0,
            0.0,
        ).astype(BF)
        seen = jnp.zeros((buckets, 1), F32)
        kept = [jnp.zeros((buckets, count), F32) for _ in range(CAP)]
        weight = [jnp.zeros((buckets, count), F32) for _ in range(CAP)]
        for k in range(top):
            ones = jnp.where(bucket == routes[k : k + 1, :] * n_rep + serve, 1.0, 0.0)
            slot_of = dot(ones.astype(BF), earlier) + seen
            seen = seen + jnp.sum(ones, axis=1, keepdims=True)
            gate = gates[k : k + 1, :]
            for slot in range(CAP):
                here = jnp.where((slot_of == float(slot)) & (limit > float(slot)), ones, 0.0)
                kept[slot] = kept[slot] + here
                weight[slot] = weight[slot] + here * gate
        for slot in range(CAP):
            taken = slice(slot * buckets, (slot + 1) * buckets)
            high = weight[slot].astype(BF)
            pick[taken, :] = kept[slot].astype(BF)
            pick_hi[taken, :] = high
            pick_lo[taken, :] = (weight[slot] - high.astype(F32)).astype(BF)

    def gather(array):
        for slot in range(CAP):
            taken = slice(slot * buckets, (slot + 1) * buckets)
            if array == 0:
                picked = dot(pick[taken, :], token_rows[...])
            else:
                picked = dot(pick_hi[taken, :], cotangent_rows[...]) + dot(pick_lo[taken, :], cotangent_rows[...])
            pack(stage, slot, picked, buckets, tiles)
        leave[array] = stage[...].astype(BF).reshape(leave.shape[1:])

    with jax.named_scope("gather_rows"):
        for array in range(2):
            loads[array].wait()
            gather(array)

    weights = (
        (lambda h: w_gate.at[:, hid[h]], lambda q, h: all_gate.at[q, :, hid[h]]),
        (lambda h: w_up.at[:, hid[h]], lambda q, h: all_up.at[q, :, hid[h]]),
        (lambda h: w_down.at[hid[h], :], lambda q, h: all_down.at[q, hid[h], :]),
    )
    half_views = (
        lambda q, h, side: all_gate.at[q, halves[side], hid[h]],
        lambda q, h, side: all_up.at[q, halves[side], hid[h]],
        lambda q, h, side: all_down.at[
            q, slice(hid[h].start + side * HID_CHUNKS[h] // 2, hid[h].start + (side + 1) * HID_CHUNKS[h] // 2), :
        ],
    )

    def weight_copy(h, kind, side):
        source, target = weights[kind]
        return remote(
            source(h), target(my_rep, h), [weight_sem.at[h, kind, side, i] for i in range(2)], {"rep": beside[side]}
        )

    def relay_copy(h, kind, side):
        block = half_views[kind](beside[1 - side], h, side)
        return remote(block, block, [weight_sem.at[h, kind, side, 2 + i] for i in range(2)], {"rep": beside[side]})

    every = [(kind, side) for kind in range(3) for side in range(2)]

    def send_weights(h):
        for kind, side in every:
            weight_copy(h, kind, side).start()

    def relay_weights(h):
        for kind, side in every:
            weight_copy(h, kind, side).wait_recv()
            relay_copy(h, kind, side).start()

    def wait_weights(h, kinds):
        for kind in kinds:
            for side in range(2):
                relay_copy(h, kind, side).wait_recv()

    def exchange(source, target, sem):
        def send(dp, rep):
            remote(
                source.at[dp * n_rep + rep], target.at[me], (sem.at[0], sem.at[1]), {"dp": dp, "rep": rep}
            ).start()

        to_others(send)
        target[me] = source[me]

    def wait_exchange(target, sem):
        wait_for(target.at[pl.ds(0, buckets - 1)], sem)

    def take_rows(array):
        wait_exchange(arrive.at[array], row_sem.at[array, 1])
        stage[...] = arrive[array].astype(F32).reshape(stage.shape)
        for slot in range(CAP):
            for tile in range(tiles):
                rows[array, slot * buckets : (slot + 1) * buckets, tile * LANES : (tile + 1) * LANES] = unpack(
                    stage, slot, tile, buckets, tiles
                ).astype(BF)

    def part_copy(h, group, phase):
        source = (part.at[groups[group], theirs, hid[h]], part.at[groups[group], mine, hid[h]], cross.at[groups[group], :, hid[h]])
        return remote(
            source[phase],
            inbox.at[phase, groups[group], :, hid[h]],
            [part_sem.at[h, group, phase, i] for i in range(2)],
            {"ctx": opposite if phase == 2 else partner},
        )

    def send_part(h, group):
        if group == 0:
            for kind, full in enumerate((all_gate, all_up)):
                part[kind, :, hid[h]] = dot(rows[0], full[:, :, hid[h]].reshape(width, HID_CHUNKS[h])).astype(BF)
        else:
            part[2, :, hid[h]] = sum(
                dot_last(rows[1, :, q * piece : (q + 1) * piece], all_down[q, hid[h], :]) for q in range(n_rep)
            ).astype(BF)

        @pl.when(outer)
        def _():
            part_copy(h, group, 0).start()
            part_copy(h, group, 1).start()

    def cross_part(h, group):
        @pl.when(inner)
        def _():
            part_copy(h, group, 0).wait_recv()
            for kind in range(3)[groups[group]]:
                cross[kind, :, hid[h]] = (
                    part[kind, theirs, hid[h]].astype(F32) + inbox[0, kind, :, hid[h]].astype(F32)
                ).astype(BF)
            part_copy(h, group, 2).start()

    def summed(h, kind):
        return (
            part[kind, mine, hid[h]].astype(F32)
            + inbox[1, kind, :, hid[h]].astype(F32)
            + inbox[2, kind, :, hid[h]].astype(F32)
        )

    def act_copy(h, group, phase):
        block = act.at[act_groups[group], theirs if phase == 2 else mine, hid[h]]
        return remote(
            block,
            block,
            [act_sem.at[h, group, phase, i] for i in range(2)],
            {"ctx": opposite if phase == 0 else partner},
        )

    def activate(h, group):
        @pl.when(inner)
        def _():
            part_copy(h, group, 1).wait_recv()
            part_copy(h, group, 2).wait_recv()
            pre_gate, pre_up = summed(h, 0), summed(h, 1)
            sigmoid = jax.nn.sigmoid(pre_gate)
            swish = pre_gate * sigmoid
            if group == 0:
                act[0, mine, hid[h]] = (swish * pre_up).astype(BF)
            else:
                grad = summed(h, 2)
                act[1, mine, hid[h]] = (grad * pre_up * sigmoid * (1.0 + pre_gate * (1.0 - sigmoid))).astype(BF)
                act[2, mine, hid[h]] = (grad * swish).astype(BF)
            act_copy(h, group, 0).start()
            act_copy(h, group, 1).start()

    def relay_act(h, group):
        @pl.when(inner)
        def _():
            act_copy(h, group, 0).wait_recv()
            act_copy(h, group, 2).start()

    def wait_act(h, group):
        @pl.when(outer)
        def _():
            act_copy(h, group, 1).wait_recv()
            act_copy(h, group, 2).wait_recv()

    def add_outputs(h, array):
        for q in range(n_rep):
            columns = slice(q * piece, (q + 1) * piece)
            if array == 0:
                term = dot(act[0, :, hid[h]], all_down[q, hid[h], :])
            else:
                term = dot_last(act[1, :, hid[h]], all_gate[q, :, hid[h]]) + dot_last(
                    act[2, :, hid[h]], all_up[q, :, hid[h]]
                )
            total[array, :, columns] = term + total[array, :, columns] if h else term

    def send_outputs(array):
        for slot in range(CAP):
            pack(stage, slot, total[array, slot * buckets : (slot + 1) * buckets, :], buckets, tiles)
        back_leave[array] = stage[...].astype(BF).reshape(back_leave.shape[1:])
        exchange(back_leave.at[array], back_arrive.at[array], back_sem.at[array])

    def combine(array):
        wait_exchange(back_arrive.at[array], back_sem.at[array, 1])
        stage[...] = back_arrive[array].astype(F32).reshape(stage.shape)
        for tile in range(tiles):
            block = jnp.concatenate(
                [unpack(stage, slot, tile, buckets, tiles) for slot in range(CAP)], axis=0
            ).astype(BF)
            columns = slice(tile * LANES, (tile + 1) * LANES)
            if array == 0:
                out_rows[0, :, columns] = (dot_first(pick_hi[...], block) + dot_first(pick_lo[...], block)).astype(BF)
            else:
                out_rows[1, :, columns] = dot_first(pick[...], block).astype(BF)
        row_out(array).start()

    def row_out(array):
        return pltpu.make_async_copy(out_rows.at[array], (layer_out, input_grad)[array], out_sem.at[array])

    def grad_out(h, kind):
        source = (out_tall.at[0, :, hid[h]], out_tall.at[1, :, hid[h]], out_wide.at[hid[h], :])
        target = (grad_gate.at[:, hid[h]], grad_up.at[:, hid[h]], grad_down.at[hid[h], :])
        return pltpu.make_async_copy(source[kind], target[kind], out_sem.at[2 + 3 * h + kind])

    def grad_relay_copy(h, side):
        return remote(
            grad_part.at[across, :, halves[side], hid[h]],
            grad_relay.at[side, :, :, hid[h]],
            [relay_sem.at[h, side, i] for i in range(2)],
            {"rep": beside[side]},
        )

    def grad_copy(h, side):
        return remote(
            grad_part.at[beside[side], :, :, hid[h]],
            grad_in.at[side, :, :, hid[h]],
            [grad_sem.at[h, side, i] for i in range(2)],
            {"rep": beside[side]},
        )

    def make_grads(h):
        for q in range(n_rep):
            columns = slice(q * piece, (q + 1) * piece)
            for kind, (array, by) in enumerate(((0, 1), (0, 2), (1, 0))):
                grad_part[q, kind, :, hid[h]] = dot_first(rows[array, :, columns], act[by, :, hid[h]]).astype(BF)
        for side in range(2):
            grad_relay_copy(h, side).start()

    def pass_grads(h):
        for side in range(2):
            grad_relay_copy(h, side).wait_recv()
            grad_part[beside[side], :, halves[side], hid[h]] = (
                grad_part[beside[side], :, halves[side], hid[h]].astype(F32)
                + grad_relay[side, :, :, hid[h]].astype(F32)
            ).astype(BF)
            grad_copy(h, side).start()

    def add_grads(h):
        for side in range(2):
            grad_copy(h, side).wait_recv()
        for kind in range(3):
            full = (
                grad_part[my_rep, kind, :, hid[h]].astype(F32)
                + grad_in[0, kind, :, hid[h]].astype(F32)
                + grad_in[1, kind, :, hid[h]].astype(F32)
            )
            if kind < 2:
                out_tall[kind, :, hid[h]] = full.astype(BF)
            else:
                out_wide[hid[h], :] = full.T.astype(BF)
            grad_out(h, kind).start()

    with jax.named_scope("entry"):
        pl.semaphore_wait(barrier, buckets - 1 + n_ctx - 1)
    with jax.named_scope("issue"):
        send_weights(0)
        exchange(leave.at[0], arrive.at[0], row_sem.at[0])
        exchange(leave.at[1], arrive.at[1], row_sem.at[1])
        send_weights(1)
        send_weights(2)
        for copy in loads[2:]:
            copy.wait()

    def step(name, call, *args):
        with jax.named_scope(name):
            call(*args)

    def grads_and_outputs(h):
        wait_act(h, 0)
        wait_act(h, 1)
        make_grads(h)
        add_outputs(h, 0)
        add_outputs(h, 1)

    step("relay_0", relay_weights, 0)
    step("tokens", take_rows, 0)
    step("weights_0a", wait_weights, 0, (0, 1))
    step("part_0a", send_part, 0, 0)
    step("cross_0a", cross_part, 0, 0)
    step("relay_1", relay_weights, 1)
    step("scaled", take_rows, 1)
    step("weights_0b", wait_weights, 0, (2,))
    step("part_0b", send_part, 0, 1)
    step("activate_0a", activate, 0, 0)
    step("cross_0b", cross_part, 0, 1)
    step("relay_2", relay_weights, 2)
    step("weights_1", wait_weights, 1, (0, 1, 2))
    step("part_1a", send_part, 1, 0)
    step("part_1b", send_part, 1, 1)
    step("activate_0b", activate, 0, 1)
    step("act_0a", relay_act, 0, 0)
    step("cross_1a", cross_part, 1, 0)
    step("cross_1b", cross_part, 1, 1)
    step("act_0b", relay_act, 0, 1)
    step("activate_1a", activate, 1, 0)
    step("activate_1b", activate, 1, 1)
    step("weights_2", wait_weights, 2, (0, 1, 2))
    step("part_2a", send_part, 2, 0)
    step("part_2b", send_part, 2, 1)
    step("grads_0", grads_and_outputs, 0)
    step("act_1a", relay_act, 1, 0)
    step("act_1b", relay_act, 1, 1)
    step("cross_2a", cross_part, 2, 0)
    step("cross_2b", cross_part, 2, 1)
    step("grads_1", grads_and_outputs, 1)
    step("activate_2a", activate, 2, 0)
    step("activate_2b", activate, 2, 1)
    step("pass_0", pass_grads, 0)
    step("act_2a", relay_act, 2, 0)
    step("act_2b", relay_act, 2, 1)
    step("wait_2a", wait_act, 2, 0)
    step("outputs_a", add_outputs, 2, 0)
    step("return_a", send_outputs, 0)
    step("wait_2b", wait_act, 2, 1)
    step("outputs_b", add_outputs, 2, 1)
    step("return_b", send_outputs, 1)
    step("pass_1", pass_grads, 1)
    step("grads_2", make_grads, 2)
    step("add_0", add_grads, 0)
    step("pass_2", pass_grads, 2)
    step("add_1", add_grads, 1)
    step("combine_a", combine, 0)
    step("combine_b", combine, 1)
    step("add_2", add_grads, 2)

    with jax.named_scope("drain"):
        for array in range(2):
            wait_exchange(arrive.at[array], row_sem.at[array, 0])
            wait_exchange(back_arrive.at[array], back_sem.at[array, 0])
            row_out(array).wait()
        for h in range(chunks):
            for kind, side in every:
                weight_copy(h, kind, side).wait_send()
                relay_copy(h, kind, side).wait_send()
            for side in range(2):
                grad_relay_copy(h, side).wait_send()
                grad_copy(h, side).wait_send()
            for kind in range(3):
                grad_out(h, kind).wait()

        @pl.when(outer)
        def _():
            for h in range(chunks):
                for group in range(2):
                    for phase in range(2):
                        part_copy(h, group, phase).wait_send()

        @pl.when(inner)
        def _():
            for h in range(chunks):
                for group in range(2):
                    part_copy(h, group, 2).wait_send()
                    for phase in range(3):
                        act_copy(h, group, phase).wait_send()


def finish_kernel(*refs):
    count = (len(refs) - 1) // 2
    copies = [pltpu.make_async_copy(refs[i], refs[count + i], refs[-1].at[i]) for i in range(count)]
    for copy in copies:
        copy.start()
    for copy in copies:
        copy.wait()


def per_device(n_dp, n_ctx, n_rep, tokens, cotangent, routes, gates, replica_of, capacity, w_gate, w_up, w_down):
    count, width = tokens.shape
    buckets = n_dp * n_rep
    slots = CAP * buckets
    lines = CAP * (width // LANES)
    piece = width // n_rep
    hidden = w_gate.shape[2]
    chunks = len(HID_CHUNKS)
    vmem = pl.BlockSpec(memory_space=pltpu.VMEM)
    smem = pl.BlockSpec(memory_space=pltpu.SMEM)
    hbm = pl.BlockSpec(memory_space=pl.ANY)
    outs = (
        jax.ShapeDtypeStruct((count, width), BF),
        jax.ShapeDtypeStruct((count, width), BF),
        jax.ShapeDtypeStruct((piece, hidden), BF),
        jax.ShapeDtypeStruct((piece, hidden), BF),
        jax.ShapeDtypeStruct((hidden, piece), BF),
    )
    results = pl.pallas_call(
        functools.partial(expert_kernel, n_dp, n_ctx, n_rep),
        out_shape=outs,
        in_specs=[smem, smem, vmem, vmem, hbm, hbm, hbm, hbm, hbm],
        out_specs=[hbm] * 5,
        scratch_shapes=[
            pltpu.VMEM((count, width), BF),
            pltpu.VMEM((count, width), BF),
            pltpu.VMEM((slots, count), BF),
            pltpu.VMEM((slots, count), BF),
            pltpu.VMEM((slots, count), BF),
            pltpu.VMEM((2, buckets, lines, LANES), BF),
            pltpu.VMEM((2, buckets, lines, LANES), BF),
            pltpu.VMEM((2, buckets, lines, LANES), BF),
            pltpu.VMEM((2, buckets, lines, LANES), BF),
            pltpu.VMEM((n_rep, piece, hidden), BF),
            pltpu.VMEM((n_rep, piece, hidden), BF),
            pltpu.VMEM((n_rep, hidden, piece), BF),
            pltpu.VMEM((buckets * lines, LANES), F32),
            pltpu.VMEM((2, slots, width), BF),
            pltpu.VMEM((3, slots, hidden), BF),
            pltpu.VMEM((3, 3, slots // 2, hidden), BF),
            pltpu.VMEM((3, slots // 2, hidden), BF),
            pltpu.VMEM((3, slots, hidden), BF),
            pltpu.VMEM((2, slots, width), F32),
            pltpu.VMEM((n_rep, 3, piece, hidden), BF),
            pltpu.VMEM((2, 3, piece // 2, hidden), BF),
            pltpu.VMEM((2, 3, piece, hidden), BF),
            pltpu.VMEM((2, count, width), BF),
            pltpu.VMEM((2, piece, hidden), BF),
            pltpu.VMEM((hidden, piece), BF),
            pltpu.SemaphoreType.DMA((5,)),
            pltpu.SemaphoreType.DMA((2, 2)),
            pltpu.SemaphoreType.DMA((chunks, 3, 2, 4)),
            pltpu.SemaphoreType.DMA((chunks, 2, 3, 2)),
            pltpu.SemaphoreType.DMA((chunks, 2, 3, 2)),
            pltpu.SemaphoreType.DMA((2, 2)),
            pltpu.SemaphoreType.DMA((chunks, 2, 2)),
            pltpu.SemaphoreType.DMA((chunks, 2, 2)),
            pltpu.SemaphoreType.DMA((2 + 3 * chunks,)),
        ],
        compiler_params=pltpu.CompilerParams(
            vmem_limit_bytes=VMEM_BYTES, collective_id=0, has_side_effects=True
        ),
        name="experts",
    )(replica_of, capacity, routes.T, gates.T, tokens, cotangent, w_gate[0], w_up[0], w_down[0])
    layer_out, input_grad, grad_gate, grad_up, grad_down = pl.pallas_call(
        finish_kernel,
        out_shape=outs,
        in_specs=[vmem] * 5,
        out_specs=[hbm] * 5,
        scratch_shapes=[pltpu.SemaphoreType.DMA((5,))],
        name="finish",
    )(*results)
    return layer_out, input_grad, grad_gate[None], grad_up[None], grad_down[None]


def solution(mesh):
    rows = P(("dp", "rep"), "ctx")
    routed = P(("dp", "rep"), None)
    tall = P("dp", ("ctx", "rep"), None)
    wide = P("dp", None, ("ctx", "rep"))
    sizes = dict(mesh.shape)
    return jax.shard_map(
        functools.partial(per_device, sizes["dp"], sizes["ctx"], sizes["rep"]),
        mesh=mesh,
        in_specs=(rows, rows, routed, routed, P(("dp", "rep")), P(), tall, tall, wide),
        out_specs=(rows, rows, tall, tall, wide),
        check_vma=False,
    )
```

```python
import functools

import jax
import jax.numpy as jnp
from jax import lax
from jax.experimental import pallas as pl
from jax.experimental.pallas import tpu as pltpu
from jax.sharding import PartitionSpec as P

MESH = pl.DeviceIdType.MESH
BF = jnp.bfloat16
F32 = jnp.float32
BLK = 16
CAP = 2
LANES = 128
HID_CHUNKS = (384, 256, 128)
VMEM_BYTES = 58 * 1024 * 1024


def dot(left, right):
    return jnp.dot(left, right, preferred_element_type=F32)


def dot_first(left, right):
    return lax.dot_general(left, right, (((0,), (0,)), ((), ())), preferred_element_type=F32)


def dot_last(left, right):
    return lax.dot_general(left, right, (((1,), (1,)), ((), ())), preferred_element_type=F32)


def pack(stage, slot, rows, buckets, tiles):
    for tile in range(tiles):
        stage[pl.ds(slot * tiles + tile, buckets, stride=CAP * tiles), :] = rows[:, tile * LANES : (tile + 1) * LANES]


def unpack(stage, slot, tile, buckets, tiles):
    return stage[pl.ds(slot * tiles + tile, buckets, stride=CAP * tiles), :]


def expert_kernel(
    n_dp,
    n_ctx,
    n_rep,
    replica,
    capacity,
    routes,
    gates,
    tokens,
    cotangent,
    w_gate,
    w_up,
    w_down,
    layer_out,
    input_grad,
    grad_gate,
    grad_up,
    grad_down,
    token_rows,
    cotangent_rows,
    pick,
    pick_hi,
    pick_lo,
    leave,
    arrive,
    back_leave,
    back_arrive,
    all_gate,
    all_up,
    all_down,
    stage,
    rows,
    part,
    inbox,
    cross,
    act,
    total,
    grad_part,
    grad_relay,
    grad_in,
    out_rows,
    out_tall,
    out_wide,
    local_sem,
    row_sem,
    weight_sem,
    part_sem,
    act_sem,
    back_sem,
    relay_sem,
    grad_sem,
    out_sem,
    column_sem,
):
    buckets = n_dp * n_rep
    my_dp, my_ctx, my_rep = (lax.axis_index(name) for name in ("dp", "ctx", "rep"))
    me = my_dp * n_rep + my_rep
    right, left = lax.rem(my_rep + 1, n_rep), lax.rem(my_rep + n_rep - 1, n_rep)
    beside = (right, left)
    across = lax.rem(my_rep + 2, n_rep)
    count, width = tokens.shape
    top = routes.shape[0]
    tiles = width // LANES
    piece = width // n_rep
    chunks = len(HID_CHUNKS)
    ends = [sum(HID_CHUNKS[: h + 1]) for h in range(chunks)]
    hid = [slice(end - size, end) for end, size in zip(ends, HID_CHUNKS)]
    share = rows.shape[1] // 2
    inner = jnp.logical_or(my_ctx == 1, my_ctx == 2)
    outer = jnp.logical_not(inner)
    partner = my_ctx + 1 - 2 * lax.rem(my_ctx, 2)
    opposite = n_ctx - 1 - my_ctx
    mine = pl.ds(pl.multiple_of((my_ctx // 2) * share, share), share)
    theirs = pl.ds(pl.multiple_of((1 - my_ctx // 2) * share, share), share)
    groups = (slice(0, 2), slice(2, 3))
    act_groups = (slice(0, 1), slice(1, 3))
    halves = (slice(0, piece // 2), slice(piece // 2, piece))

    def remote(source, target, sem, where):
        return pltpu.make_async_remote_copy(
            src_ref=source,
            dst_ref=target,
            send_sem=sem[0],
            recv_sem=sem[1],
            device_id=where,
            device_id_type=MESH,
        )

    def wait_for(view, sem):
        pltpu.make_async_copy(view, view, sem).wait()

    barrier = pltpu.get_barrier_semaphore()

    reps = [lax.rem(my_rep + step, n_rep) for step in range(n_rep)]

    def to_others(visit):
        def one(step, carry):
            other = lax.rem(my_dp + step, n_dp)
            for rep in reps:
                visit(other, rep)
            return carry

        lax.fori_loop(1, n_dp, one, 0)
        for rep in reps[1:]:
            visit(my_dp, rep)

    def greet(dp, rep):
        pl.semaphore_signal(barrier, inc=1, device_id={"dp": dp, "rep": rep}, device_id_type=MESH)

    with jax.named_scope("greet"):
        def greet_column(step, carry):
            greet(lax.rem(my_dp + step, n_dp), my_rep)
            return carry

        lax.fori_loop(1, n_dp, greet_column, 0)
        for rep in reps[1:]:
            greet(my_dp, rep)
        for step in range(1, n_ctx):
            pl.semaphore_signal(
                barrier, inc=1, device_id={"ctx": lax.rem(my_ctx + step, n_ctx)}, device_id_type=MESH
            )
        loads = [
            pltpu.make_async_copy(source, target, local_sem.at[kind])
            for kind, (source, target) in enumerate(
                (
                    (tokens, token_rows),
                    (cotangent, cotangent_rows),
                    (w_gate, all_gate.at[my_rep]),
                    (w_up, all_up.at[my_rep]),
                    (w_down, all_down.at[my_rep]),
                )
            )
        ]
        for copy in loads:
            copy.start()

    with jax.named_scope("slots"):
        token = lax.broadcasted_iota(jnp.int32, (1, count), 1)
        serve = jnp.zeros((1, count), jnp.int32)
        for block in range(count // BLK):
            serve = jnp.where(token // BLK == block, replica[block], serve)
        bucket = lax.broadcasted_iota(jnp.int32, (buckets, 1), 0)
        limit = jnp.zeros((buckets, 1), jnp.int32)
        for expert in range(n_dp):
            limit = jnp.where(bucket // n_rep == expert, capacity[expert], limit)
        limit = limit.astype(F32)
        bucket = lax.broadcasted_iota(jnp.int32, (buckets, count), 0)
        earlier = jnp.where(
            lax.broadcasted_iota(jnp.int32, (count, count), 0) < lax.broadcasted_iota(jnp.int32, (count, count), 1),
            1.0,
            0.0,
        ).astype(BF)
        seen = jnp.zeros((buckets, 1), F32)
        kept = [jnp.zeros((buckets, count), F32) for _ in range(CAP)]
        weight = [jnp.zeros((buckets, count), F32) for _ in range(CAP)]
        for k in range(top):
            ones = jnp.where(bucket == routes[k : k + 1, :] * n_rep + serve, 1.0, 0.0)
            slot_of = dot(ones.astype(BF), earlier) + seen
            seen = seen + jnp.sum(ones, axis=1, keepdims=True)
            gate = gates[k : k + 1, :]
            for slot in range(CAP):
                here = jnp.where((slot_of == float(slot)) & (limit > float(slot)), ones, 0.0)
                kept[slot] = kept[slot] + here
                weight[slot] = weight[slot] + here * gate
        for slot in range(CAP):
            taken = slice(slot * buckets, (slot + 1) * buckets)
            high = weight[slot].astype(BF)
            pick[taken, :] = kept[slot].astype(BF)
            pick_hi[taken, :] = high
            pick_lo[taken, :] = (weight[slot] - high.astype(F32)).astype(BF)

    def gather(array):
        for slot in range(CAP):
            taken = slice(slot * buckets, (slot + 1) * buckets)
            if array == 0:
                picked = dot(pick[taken, :], token_rows[...])
            else:
                picked = dot(pick_hi[taken, :], cotangent_rows[...]) + dot(pick_lo[taken, :], cotangent_rows[...])
            pack(stage, slot, picked, buckets, tiles)
        leave[array] = stage[...].astype(BF).reshape(leave.shape[1:])

    weights = (
        (lambda h: w_gate.at[:, hid[h]], lambda q, h: all_gate.at[q, :, hid[h]]),
        (lambda h: w_up.at[:, hid[h]], lambda q, h: all_up.at[q, :, hid[h]]),
        (lambda h: w_down.at[hid[h], :], lambda q, h: all_down.at[q, hid[h], :]),
    )
    half_views = (
        lambda q, h, side: all_gate.at[q, halves[side], hid[h]],
        lambda q, h, side: all_up.at[q, halves[side], hid[h]],
        lambda q, h, side: all_down.at[
            q, slice(hid[h].start + side * HID_CHUNKS[h] // 2, hid[h].start + (side + 1) * HID_CHUNKS[h] // 2), :
        ],
    )

    def weight_copy(h, kind, side):
        source, target = weights[kind]
        return remote(
            source(h), target(my_rep, h), [weight_sem.at[h, kind, side, i] for i in range(2)], {"rep": beside[side]}
        )

    def relay_copy(h, kind, side):
        block = half_views[kind](beside[1 - side], h, side)
        return remote(block, block, [weight_sem.at[h, kind, side, 2 + i] for i in range(2)], {"rep": beside[side]})

    every = [(kind, side) for kind in range(3) for side in range(2)]

    def send_weights(h):
        for kind, side in every:
            weight_copy(h, kind, side).start()

    def relay_weights(h):
        for kind, side in every:
            weight_copy(h, kind, side).wait_recv()
            relay_copy(h, kind, side).start()

    def wait_weights(h, kinds):
        for kind in kinds:
            for side in range(2):
                relay_copy(h, kind, side).wait_recv()

    def exchange(source, target, sem):
        def send(dp, rep):
            remote(
                source.at[dp * n_rep + rep], target.at[me], (sem.at[0], sem.at[1]), {"dp": dp, "rep": rep}
            ).start()

        to_others(send)
        target[me] = source[me]

    def wait_exchange(target, sem):
        wait_for(target.at[pl.ds(0, buckets - 1)], sem)

    def take_rows(array):
        wait_exchange(arrive.at[array], row_sem.at[array, 1])
        stage[...] = arrive[array].astype(F32).reshape(stage.shape)
        for slot in range(CAP):
            for tile in range(tiles):
                rows[array, slot * buckets : (slot + 1) * buckets, tile * LANES : (tile + 1) * LANES] = unpack(
                    stage, slot, tile, buckets, tiles
                ).astype(BF)

    def part_copy(h, group, phase):
        source = (part.at[groups[group], theirs, hid[h]], part.at[groups[group], mine, hid[h]], cross.at[groups[group], :, hid[h]])
        return remote(
            source[phase],
            inbox.at[phase, groups[group], :, hid[h]],
            [part_sem.at[h, group, phase, i] for i in range(2)],
            {"ctx": opposite if phase == 2 else partner},
        )

    def send_part(h, group):
        if group == 0:
            for kind, full in enumerate((all_gate, all_up)):
                part[kind, :, hid[h]] = dot(rows[0], full[:, :, hid[h]].reshape(width, HID_CHUNKS[h])).astype(BF)
        else:
            part[2, :, hid[h]] = sum(
                dot_last(rows[1, :, q * piece : (q + 1) * piece], all_down[q, hid[h], :]) for q in range(n_rep)
            ).astype(BF)

        @pl.when(outer)
        def _():
            part_copy(h, group, 0).start()
            part_copy(h, group, 1).start()

    def cross_part(h, group):
        @pl.when(inner)
        def _():
            part_copy(h, group, 0).wait_recv()
            for kind in range(3)[groups[group]]:
                cross[kind, :, hid[h]] = (
                    part[kind, theirs, hid[h]].astype(F32) + inbox[0, kind, :, hid[h]].astype(F32)
                ).astype(BF)
            part_copy(h, group, 2).start()

    def summed(h, kind):
        return (
            part[kind, mine, hid[h]].astype(F32)
            + inbox[1, kind, :, hid[h]].astype(F32)
            + inbox[2, kind, :, hid[h]].astype(F32)
        )

    def act_copy(h, group, phase):
        block = act.at[act_groups[group], theirs if phase == 2 else mine, hid[h]]
        return remote(
            block,
            block,
            [act_sem.at[h, group, phase, i] for i in range(2)],
            {"ctx": opposite if phase == 0 else partner},
        )

    def activate(h, group):
        @pl.when(inner)
        def _():
            part_copy(h, group, 1).wait_recv()
            part_copy(h, group, 2).wait_recv()
            pre_gate, pre_up = summed(h, 0), summed(h, 1)
            sigmoid = jax.nn.sigmoid(pre_gate)
            swish = pre_gate * sigmoid
            if group == 0:
                act[0, mine, hid[h]] = (swish * pre_up).astype(BF)
            else:
                grad = summed(h, 2)
                act[1, mine, hid[h]] = (grad * pre_up * sigmoid * (1.0 + pre_gate * (1.0 - sigmoid))).astype(BF)
                act[2, mine, hid[h]] = (grad * swish).astype(BF)
            act_copy(h, group, 0).start()
            act_copy(h, group, 1).start()

    def relay_act(h, group):
        @pl.when(inner)
        def _():
            act_copy(h, group, 0).wait_recv()
            act_copy(h, group, 2).start()

    def wait_act(h, group):
        @pl.when(outer)
        def _():
            act_copy(h, group, 1).wait_recv()
            act_copy(h, group, 2).wait_recv()

    def add_outputs(h, array):
        for q in range(n_rep):
            columns = slice(q * piece, (q + 1) * piece)
            if array == 0:
                term = dot(act[0, :, hid[h]], all_down[q, hid[h], :])
            else:
                term = dot_last(act[1, :, hid[h]], all_gate[q, :, hid[h]]) + dot_last(
                    act[2, :, hid[h]], all_up[q, :, hid[h]]
                )
            total[array, :, columns] = term + total[array, :, columns] if h else term

    def send_outputs(array):
        for slot in range(CAP):
            pack(stage, slot, total[array, slot * buckets : (slot + 1) * buckets, :], buckets, tiles)
        back_leave[array] = stage[...].astype(BF).reshape(back_leave.shape[1:])
        exchange(back_leave.at[array], back_arrive.at[array], back_sem.at[array])

    def combine(array):
        wait_exchange(back_arrive.at[array], back_sem.at[array, 1])
        stage[...] = back_arrive[array].astype(F32).reshape(stage.shape)
        for tile in range(tiles):
            block = jnp.concatenate(
                [unpack(stage, slot, tile, buckets, tiles) for slot in range(CAP)], axis=0
            ).astype(BF)
            columns = slice(tile * LANES, (tile + 1) * LANES)
            if array == 0:
                out_rows[0, :, columns] = (dot_first(pick_hi[...], block) + dot_first(pick_lo[...], block)).astype(BF)
            else:
                out_rows[1, :, columns] = dot_first(pick[...], block).astype(BF)
        row_out(array).start()

    def row_out(array):
        return pltpu.make_async_copy(out_rows.at[array], (layer_out, input_grad)[array], out_sem.at[array])

    def grad_out(h, kind):
        source = (out_tall.at[0, :, hid[h]], out_tall.at[1, :, hid[h]], out_wide.at[hid[h], :])
        target = (grad_gate.at[:, hid[h]], grad_up.at[:, hid[h]], grad_down.at[hid[h], :])
        return pltpu.make_async_copy(source[kind], target[kind], out_sem.at[2 + 3 * h + kind])

    def grad_relay_copy(h, side):
        return remote(
            grad_part.at[across, :, halves[side], hid[h]],
            grad_relay.at[side, :, :, hid[h]],
            [relay_sem.at[h, side, i] for i in range(2)],
            {"rep": beside[side]},
        )

    def grad_copy(h, side):
        return remote(
            grad_part.at[beside[side], :, :, hid[h]],
            grad_in.at[side, :, :, hid[h]],
            [grad_sem.at[h, side, i] for i in range(2)],
            {"rep": beside[side]},
        )

    def make_grads(h):
        for q in range(n_rep):
            columns = slice(q * piece, (q + 1) * piece)
            for kind, (array, by) in enumerate(((0, 1), (0, 2), (1, 0))):
                grad_part[q, kind, :, hid[h]] = dot_first(rows[array, :, columns], act[by, :, hid[h]]).astype(BF)
        for side in range(2):
            grad_relay_copy(h, side).start()

    def pass_grads(h):
        for side in range(2):
            grad_relay_copy(h, side).wait_recv()
            grad_part[beside[side], :, halves[side], hid[h]] = (
                grad_part[beside[side], :, halves[side], hid[h]].astype(F32)
                + grad_relay[side, :, :, hid[h]].astype(F32)
            ).astype(BF)
            grad_copy(h, side).start()

    def add_grads(h):
        for side in range(2):
            grad_copy(h, side).wait_recv()
        for kind in range(3):
            full = (
                grad_part[my_rep, kind, :, hid[h]].astype(F32)
                + grad_in[0, kind, :, hid[h]].astype(F32)
                + grad_in[1, kind, :, hid[h]].astype(F32)
            )
            if kind < 2:
                out_tall[kind, :, hid[h]] = full.astype(BF)
            else:
                out_wide[hid[h], :] = full.T.astype(BF)
            grad_out(h, kind).start()

    with jax.named_scope("entry"):
        pl.semaphore_wait(barrier, n_dp - 1 + n_rep - 1 + n_ctx - 1)
    with jax.named_scope("first_weights"):
        for rep in reps[1:]:
            pl.semaphore_signal(column_sem, inc=1, device_id={"rep": rep}, device_id_type=MESH)
        send_weights(0)
    with jax.named_scope("gather_rows"):
        for array in range(2):
            loads[array].wait()
            gather(array)

    with jax.named_scope("issue"):
        pl.semaphore_wait(column_sem, n_rep - 1)
        exchange(leave.at[0], arrive.at[0], row_sem.at[0])
        exchange(leave.at[1], arrive.at[1], row_sem.at[1])
        for copy in loads[2:]:
            copy.wait()

    def step(name, call, *args):
        with jax.named_scope(name):
            call(*args)

    def grads_and_outputs(h):
        wait_act(h, 0)
        wait_act(h, 1)
        make_grads(h)
        add_outputs(h, 0)
        add_outputs(h, 1)

    step("relay_0", relay_weights, 0)
    step("weights_to_1", send_weights, 1)
    step("tokens", take_rows, 0)
    step("weights_0a", wait_weights, 0, (0, 1))
    step("part_0a", send_part, 0, 0)
    step("cross_0a", cross_part, 0, 0)
    step("relay_1", relay_weights, 1)
    step("weights_to_2", send_weights, 2)
    step("scaled", take_rows, 1)
    step("weights_0b", wait_weights, 0, (2,))
    step("part_0b", send_part, 0, 1)
    step("activate_0a", activate, 0, 0)
    step("cross_0b", cross_part, 0, 1)
    step("relay_2", relay_weights, 2)
    step("weights_1", wait_weights, 1, (0, 1, 2))
    step("part_1a", send_part, 1, 0)
    step("part_1b", send_part, 1, 1)
    step("activate_0b", activate, 0, 1)
    step("act_0a", relay_act, 0, 0)
    step("cross_1a", cross_part, 1, 0)
    step("cross_1b", cross_part, 1, 1)
    step("act_0b", relay_act, 0, 1)
    step("weights_2", wait_weights, 2, (0, 1, 2))
    step("part_2a", send_part, 2, 0)
    step("part_2b", send_part, 2, 1)
    step("activate_1a", activate, 1, 0)
    step("activate_1b", activate, 1, 1)
    step("grads_0", grads_and_outputs, 0)
    step("cross_2a", cross_part, 2, 0)
    step("cross_2b", cross_part, 2, 1)
    step("act_1a", relay_act, 1, 0)
    step("act_1b", relay_act, 1, 1)
    step("activate_2a", activate, 2, 0)
    step("activate_2b", activate, 2, 1)
    step("pass_0", pass_grads, 0)
    step("grads_1", grads_and_outputs, 1)
    step("act_2a", relay_act, 2, 0)
    step("act_2b", relay_act, 2, 1)
    step("wait_2a", wait_act, 2, 0)
    step("outputs_a", add_outputs, 2, 0)
    step("return_a", send_outputs, 0)
    step("wait_2b", wait_act, 2, 1)
    step("outputs_b", add_outputs, 2, 1)
    step("pass_1", pass_grads, 1)
    step("grads_2", make_grads, 2)
    step("return_b", send_outputs, 1)
    step("pass_2", pass_grads, 2)
    step("add_0", add_grads, 0)
    step("add_1", add_grads, 1)
    step("combine_a", combine, 0)
    step("combine_b", combine, 1)
    step("add_2", add_grads, 2)

    with jax.named_scope("drain"):
        for array in range(2):
            wait_exchange(arrive.at[array], row_sem.at[array, 0])
            wait_exchange(back_arrive.at[array], back_sem.at[array, 0])
            row_out(array).wait()
        for h in range(chunks):
            for kind, side in every:
                weight_copy(h, kind, side).wait_send()
                relay_copy(h, kind, side).wait_send()
            for side in range(2):
                grad_relay_copy(h, side).wait_send()
                grad_copy(h, side).wait_send()
            for kind in range(3):
                grad_out(h, kind).wait()

        @pl.when(outer)
        def _():
            for h in range(chunks):
                for group in range(2):
                    for phase in range(2):
                        part_copy(h, group, phase).wait_send()

        @pl.when(inner)
        def _():
            for h in range(chunks):
                for group in range(2):
                    part_copy(h, group, 2).wait_send()
                    for phase in range(3):
                        act_copy(h, group, phase).wait_send()


def finish_kernel(*refs):
    count = (len(refs) - 1) // 2
    copies = [pltpu.make_async_copy(refs[i], refs[count + i], refs[-1].at[i]) for i in range(count)]
    for copy in copies:
        copy.start()
    for copy in copies:
        copy.wait()


def per_device(n_dp, n_ctx, n_rep, tokens, cotangent, routes, gates, replica_of, capacity, w_gate, w_up, w_down):
    count, width = tokens.shape
    buckets = n_dp * n_rep
    slots = CAP * buckets
    lines = CAP * (width // LANES)
    piece = width // n_rep
    hidden = w_gate.shape[2]
    chunks = len(HID_CHUNKS)
    vmem = pl.BlockSpec(memory_space=pltpu.VMEM)
    smem = pl.BlockSpec(memory_space=pltpu.SMEM)
    hbm = pl.BlockSpec(memory_space=pl.ANY)
    outs = (
        jax.ShapeDtypeStruct((count, width), BF),
        jax.ShapeDtypeStruct((count, width), BF),
        jax.ShapeDtypeStruct((piece, hidden), BF),
        jax.ShapeDtypeStruct((piece, hidden), BF),
        jax.ShapeDtypeStruct((hidden, piece), BF),
    )
    results = pl.pallas_call(
        functools.partial(expert_kernel, n_dp, n_ctx, n_rep),
        out_shape=outs,
        in_specs=[smem, smem, vmem, vmem, hbm, hbm, hbm, hbm, hbm],
        out_specs=[hbm] * 5,
        scratch_shapes=[
            pltpu.VMEM((count, width), BF),
            pltpu.VMEM((count, width), BF),
            pltpu.VMEM((slots, count), BF),
            pltpu.VMEM((slots, count), BF),
            pltpu.VMEM((slots, count), BF),
            pltpu.VMEM((2, buckets, lines, LANES), BF),
            pltpu.VMEM((2, buckets, lines, LANES), BF),
            pltpu.VMEM((2, buckets, lines, LANES), BF),
            pltpu.VMEM((2, buckets, lines, LANES), BF),
            pltpu.VMEM((n_rep, piece, hidden), BF),
            pltpu.VMEM((n_rep, piece, hidden), BF),
            pltpu.VMEM((n_rep, hidden, piece), BF),
            pltpu.VMEM((buckets * lines, LANES), F32),
            pltpu.VMEM((2, slots, width), BF),
            pltpu.VMEM((3, slots, hidden), BF),
            pltpu.VMEM((3, 3, slots // 2, hidden), BF),
            pltpu.VMEM((3, slots // 2, hidden), BF),
            pltpu.VMEM((3, slots, hidden), BF),
            pltpu.VMEM((2, slots, width), F32),
            pltpu.VMEM((n_rep, 3, piece, hidden), BF),
            pltpu.VMEM((2, 3, piece // 2, hidden), BF),
            pltpu.VMEM((2, 3, piece, hidden), BF),
            pltpu.VMEM((2, count, width), BF),
            pltpu.VMEM((2, piece, hidden), BF),
            pltpu.VMEM((hidden, piece), BF),
            pltpu.SemaphoreType.DMA((5,)),
            pltpu.SemaphoreType.DMA((2, 2)),
            pltpu.SemaphoreType.DMA((chunks, 3, 2, 4)),
            pltpu.SemaphoreType.DMA((chunks, 2, 3, 2)),
            pltpu.SemaphoreType.DMA((chunks, 2, 3, 2)),
            pltpu.SemaphoreType.DMA((2, 2)),
            pltpu.SemaphoreType.DMA((chunks, 2, 2)),
            pltpu.SemaphoreType.DMA((chunks, 2, 2)),
            pltpu.SemaphoreType.DMA((2 + 3 * chunks,)),
            pltpu.SemaphoreType.REGULAR,
        ],
        compiler_params=pltpu.CompilerParams(
            vmem_limit_bytes=VMEM_BYTES, collective_id=0, has_side_effects=True
        ),
        name="experts",
    )(replica_of, capacity, routes.T, gates.T, tokens, cotangent, w_gate[0], w_up[0], w_down[0])
    layer_out, input_grad, grad_gate, grad_up, grad_down = pl.pallas_call(
        finish_kernel,
        out_shape=outs,
        in_specs=[vmem] * 5,
        out_specs=[hbm] * 5,
        scratch_shapes=[pltpu.SemaphoreType.DMA((5,))],
        name="finish",
    )(*results)
    return layer_out, input_grad, grad_gate[None], grad_up[None], grad_down[None]


def solution(mesh):
    rows = P(("dp", "rep"), "ctx")
    routed = P(("dp", "rep"), None)
    tall = P("dp", ("ctx", "rep"), None)
    wide = P("dp", None, ("ctx", "rep"))
    sizes = dict(mesh.shape)
    return jax.shard_map(
        functools.partial(per_device, sizes["dp"], sizes["ctx"], sizes["rep"]),
        mesh=mesh,
        in_specs=(rows, rows, routed, routed, P(("dp", "rep")), P(), tall, tall, wide),
        out_specs=(rows, rows, tall, tall, wide),
        check_vma=False,
    )
```

```python
import functools

import jax
import jax.numpy as jnp
from jax import lax
from jax.experimental import pallas as pl
from jax.experimental.pallas import tpu as pltpu
from jax.sharding import PartitionSpec as P

MESH = pl.DeviceIdType.MESH
BF = jnp.bfloat16
F32 = jnp.float32
BLK = 16
CAP = 2
LANES = 128
HID_CHUNKS = (384, 256, 128)
VMEM_BYTES = 58 * 1024 * 1024


def dot(left, right):
    return jnp.dot(left, right, preferred_element_type=F32)


def dot_first(left, right):
    return lax.dot_general(left, right, (((0,), (0,)), ((), ())), preferred_element_type=F32)


def dot_last(left, right):
    return lax.dot_general(left, right, (((1,), (1,)), ((), ())), preferred_element_type=F32)


def pack(stage, slot, rows, buckets, tiles):
    for tile in range(tiles):
        stage[pl.ds(slot * tiles + tile, buckets, stride=CAP * tiles), :] = rows[:, tile * LANES : (tile + 1) * LANES]


def unpack(stage, slot, tile, buckets, tiles):
    return stage[pl.ds(slot * tiles + tile, buckets, stride=CAP * tiles), :]


def expert_kernel(
    n_dp,
    n_ctx,
    n_rep,
    replica,
    capacity,
    routes,
    gates,
    tokens,
    cotangent,
    w_gate,
    w_up,
    w_down,
    layer_out,
    input_grad,
    grad_gate,
    grad_up,
    grad_down,
    token_rows,
    cotangent_rows,
    pick,
    pick_hi,
    pick_lo,
    leave,
    arrive,
    back_leave,
    back_arrive,
    all_gate,
    all_up,
    all_down,
    stage,
    rows,
    part,
    inbox,
    cross,
    act,
    total,
    grad_part,
    grad_relay,
    grad_in,
    out_rows,
    out_tall,
    out_wide,
    local_sem,
    row_sem,
    weight_sem,
    part_sem,
    act_sem,
    back_sem,
    relay_sem,
    grad_sem,
    out_sem,
):
    buckets = n_dp * n_rep
    my_dp, my_ctx, my_rep = (lax.axis_index(name) for name in ("dp", "ctx", "rep"))
    right, left = lax.rem(my_rep + 1, n_rep), lax.rem(my_rep + n_rep - 1, n_rep)
    beside = (right, left)
    across = lax.rem(my_rep + 2, n_rep)
    count, width = tokens.shape
    top = routes.shape[0]
    tiles = width // LANES
    piece = width // n_rep
    chunks = len(HID_CHUNKS)
    ends = [sum(HID_CHUNKS[: h + 1]) for h in range(chunks)]
    hid = [slice(end - size, end) for end, size in zip(ends, HID_CHUNKS)]
    share = rows.shape[1] // 2
    inner = jnp.logical_or(my_ctx == 1, my_ctx == 2)
    outer = jnp.logical_not(inner)
    partner = my_ctx + 1 - 2 * lax.rem(my_ctx, 2)
    opposite = n_ctx - 1 - my_ctx
    mine = pl.ds(pl.multiple_of((my_ctx // 2) * share, share), share)
    theirs = pl.ds(pl.multiple_of((1 - my_ctx // 2) * share, share), share)
    groups = (slice(0, 2), slice(2, 3))
    act_groups = (slice(0, 1), slice(1, 3))
    halves = (slice(0, piece // 2), slice(piece // 2, piece))

    def remote(source, target, sem, where):
        return pltpu.make_async_remote_copy(
            src_ref=source,
            dst_ref=target,
            send_sem=sem[0],
            recv_sem=sem[1],
            device_id=where,
            device_id_type=MESH,
        )

    def wait_for(view, sem):
        pltpu.make_async_copy(view, view, sem).wait()

    barrier = pltpu.get_barrier_semaphore()

    def to_others(visit):
        def one(step, carry):
            visit(lax.rem(my_dp + step, n_dp))
            return carry

        lax.fori_loop(1, n_dp, one, 0)

    def greet(where):
        pl.semaphore_signal(barrier, inc=1, device_id=where, device_id_type=MESH)

    with jax.named_scope("greet"):
        to_others(lambda dp: greet({"dp": dp}))
        for rep in beside:
            greet({"rep": rep})
        for ctx in (partner, opposite):
            greet({"ctx": ctx})
        loads = [
            pltpu.make_async_copy(source, target, local_sem.at[kind])
            for kind, (source, target) in enumerate(
                (
                    (tokens, token_rows),
                    (cotangent, cotangent_rows),
                    (w_gate, all_gate.at[my_rep]),
                    (w_up, all_up.at[my_rep]),
                    (w_down, all_down.at[my_rep]),
                )
            )
        ]
        for copy in loads:
            copy.start()

    with jax.named_scope("slots"):
        token = lax.broadcasted_iota(jnp.int32, (1, count), 1)
        serve = jnp.zeros((1, count), jnp.int32)
        for block in range(count // BLK):
            serve = jnp.where(token // BLK == block, replica[block], serve)
        bucket = lax.broadcasted_iota(jnp.int32, (buckets, 1), 0)
        limit = jnp.zeros((buckets, 1), jnp.int32)
        for expert in range(n_dp):
            limit = jnp.where(bucket // n_rep == expert, capacity[expert], limit)
        limit = limit.astype(F32)
        bucket = lax.broadcasted_iota(jnp.int32, (buckets, count), 0)
        earlier = jnp.where(
            lax.broadcasted_iota(jnp.int32, (count, count), 0) < lax.broadcasted_iota(jnp.int32, (count, count), 1),
            1.0,
            0.0,
        ).astype(BF)
        seen = jnp.zeros((buckets, 1), F32)
        kept = [jnp.zeros((buckets, count), F32) for _ in range(CAP)]
        weight = [jnp.zeros((buckets, count), F32) for _ in range(CAP)]
        for k in range(top):
            ones = jnp.where(bucket == routes[k : k + 1, :] * n_rep + serve, 1.0, 0.0)
            slot_of = dot(ones.astype(BF), earlier) + seen
            seen = seen + jnp.sum(ones, axis=1, keepdims=True)
            gate = gates[k : k + 1, :]
            for slot in range(CAP):
                here = jnp.where((slot_of == float(slot)) & (limit > float(slot)), ones, 0.0)
                kept[slot] = kept[slot] + here
                weight[slot] = weight[slot] + here * gate
        for slot in range(CAP):
            taken = slice(slot * buckets, (slot + 1) * buckets)
            high = weight[slot].astype(BF)
            pick[taken, :] = kept[slot].astype(BF)
            pick_hi[taken, :] = high
            pick_lo[taken, :] = (weight[slot] - high.astype(F32)).astype(BF)

    def gather(array):
        for slot in range(CAP):
            taken = slice(slot * buckets, (slot + 1) * buckets)
            if array == 0:
                picked = dot(pick[taken, :], token_rows[...])
            else:
                picked = dot(pick_hi[taken, :], cotangent_rows[...]) + dot(pick_lo[taken, :], cotangent_rows[...])
            pack(stage, slot, picked, buckets, tiles)
        leave[array] = stage[...].astype(BF).reshape(leave.shape[1:])

    weights = (
        (lambda h: w_gate.at[:, hid[h]], lambda q, h: all_gate.at[q, :, hid[h]]),
        (lambda h: w_up.at[:, hid[h]], lambda q, h: all_up.at[q, :, hid[h]]),
        (lambda h: w_down.at[hid[h], :], lambda q, h: all_down.at[q, hid[h], :]),
    )
    half_views = (
        lambda q, h, side: all_gate.at[q, halves[side], hid[h]],
        lambda q, h, side: all_up.at[q, halves[side], hid[h]],
        lambda q, h, side: all_down.at[
            q, slice(hid[h].start + side * HID_CHUNKS[h] // 2, hid[h].start + (side + 1) * HID_CHUNKS[h] // 2), :
        ],
    )

    def weight_copy(h, kind, side):
        source, target = weights[kind]
        return remote(
            source(h), target(my_rep, h), [weight_sem.at[h, kind, side, i] for i in range(2)], {"rep": beside[side]}
        )

    def relay_copy(h, kind, side):
        block = half_views[kind](beside[1 - side], h, side)
        return remote(block, block, [weight_sem.at[h, kind, side, 2 + i] for i in range(2)], {"rep": beside[side]})

    every = [(kind, side) for kind in range(3) for side in range(2)]

    def send_weights(h):
        for kind, side in every:
            weight_copy(h, kind, side).start()

    def relay_weights(h):
        for kind, side in every:
            weight_copy(h, kind, side).wait_recv()
            relay_copy(h, kind, side).start()

    def wait_weights(h, kinds):
        for kind in kinds:
            for side in range(2):
                relay_copy(h, kind, side).wait_recv()

    def exchange(source, target, sem):
        def send(dp):
            remote(source.at[dp], target.at[my_dp], (sem.at[0], sem.at[1]), {"dp": dp}).start()

        to_others(send)
        target[my_dp] = source[my_dp]

    def wait_exchange(target, sem):
        wait_for(target.at[pl.ds(0, n_dp - 1)], sem)

    def take_rows(array):
        wait_exchange(arrive.at[array], row_sem.at[array, 1])
        stage[...] = arrive[array].astype(F32).reshape(stage.shape)
        for slot in range(CAP):
            for tile in range(tiles):
                rows[array, slot * buckets : (slot + 1) * buckets, tile * LANES : (tile + 1) * LANES] = unpack(
                    stage, slot, tile, buckets, tiles
                ).astype(BF)

    def part_copy(h, group, phase):
        source = (part.at[groups[group], theirs, hid[h]], part.at[groups[group], mine, hid[h]], cross.at[groups[group], :, hid[h]])
        return remote(
            source[phase],
            inbox.at[phase, groups[group], :, hid[h]],
            [part_sem.at[h, group, phase, i] for i in range(2)],
            {"ctx": opposite if phase == 2 else partner},
        )

    def send_part(h, group):
        if group == 0:
            for kind, full in enumerate((all_gate, all_up)):
                part[kind, :, hid[h]] = dot(rows[0], full[:, :, hid[h]].reshape(width, HID_CHUNKS[h])).astype(BF)
        else:
            part[2, :, hid[h]] = sum(
                dot_last(rows[1, :, q * piece : (q + 1) * piece], all_down[q, hid[h], :]) for q in range(n_rep)
            ).astype(BF)

        @pl.when(outer)
        def _():
            part_copy(h, group, 0).start()
            part_copy(h, group, 1).start()

    def cross_part(h, group):
        @pl.when(inner)
        def _():
            part_copy(h, group, 0).wait_recv()
            for kind in range(3)[groups[group]]:
                cross[kind, :, hid[h]] = (
                    part[kind, theirs, hid[h]].astype(F32) + inbox[0, kind, :, hid[h]].astype(F32)
                ).astype(BF)
            part_copy(h, group, 2).start()

    def summed(h, kind):
        return (
            part[kind, mine, hid[h]].astype(F32)
            + inbox[1, kind, :, hid[h]].astype(F32)
            + inbox[2, kind, :, hid[h]].astype(F32)
        )

    def act_copy(h, group, phase):
        block = act.at[act_groups[group], theirs if phase == 2 else mine, hid[h]]
        return remote(
            block,
            block,
            [act_sem.at[h, group, phase, i] for i in range(2)],
            {"ctx": opposite if phase == 0 else partner},
        )

    def activate(h, group):
        @pl.when(inner)
        def _():
            part_copy(h, group, 1).wait_recv()
            part_copy(h, group, 2).wait_recv()
            pre_gate, pre_up = summed(h, 0), summed(h, 1)
            sigmoid = jax.nn.sigmoid(pre_gate)
            swish = pre_gate * sigmoid
            if group == 0:
                act[0, mine, hid[h]] = (swish * pre_up).astype(BF)
            else:
                grad = summed(h, 2)
                act[1, mine, hid[h]] = (grad * pre_up * sigmoid * (1.0 + pre_gate * (1.0 - sigmoid))).astype(BF)
                act[2, mine, hid[h]] = (grad * swish).astype(BF)
            act_copy(h, group, 0).start()
            act_copy(h, group, 1).start()

    def relay_act(h, group):
        @pl.when(inner)
        def _():
            act_copy(h, group, 0).wait_recv()
            act_copy(h, group, 2).start()

    def wait_act(h, group):
        @pl.when(outer)
        def _():
            act_copy(h, group, 1).wait_recv()
            act_copy(h, group, 2).wait_recv()

    def add_outputs(h, array):
        for q in range(n_rep):
            columns = slice(q * piece, (q + 1) * piece)
            if array == 0:
                term = dot(act[0, :, hid[h]], all_down[q, hid[h], :])
            else:
                term = dot_last(act[1, :, hid[h]], all_gate[q, :, hid[h]]) + dot_last(
                    act[2, :, hid[h]], all_up[q, :, hid[h]]
                )
            total[array, :, columns] = term + total[array, :, columns] if h else term

    def send_outputs(array):
        for slot in range(CAP):
            pack(stage, slot, total[array, slot * buckets : (slot + 1) * buckets, :], buckets, tiles)
        back_leave[array] = stage[...].astype(BF).reshape(back_leave.shape[1:])
        exchange(back_leave.at[array], back_arrive.at[array], back_sem.at[array])

    def combine(array):
        wait_exchange(back_arrive.at[array], back_sem.at[array, 1])
        stage[...] = back_arrive[array].astype(F32).reshape(stage.shape)
        for tile in range(tiles):
            block = jnp.concatenate(
                [unpack(stage, slot, tile, buckets, tiles) for slot in range(CAP)], axis=0
            ).astype(BF)
            columns = slice(tile * LANES, (tile + 1) * LANES)
            if array == 0:
                out_rows[0, :, columns] = (dot_first(pick_hi[...], block) + dot_first(pick_lo[...], block)).astype(BF)
            else:
                out_rows[1, :, columns] = dot_first(pick[...], block).astype(BF)
        row_out(array).start()

    def row_out(array):
        return pltpu.make_async_copy(out_rows.at[array], (layer_out, input_grad)[array], out_sem.at[array])

    def grad_out(h, kind):
        source = (out_tall.at[0, :, hid[h]], out_tall.at[1, :, hid[h]], out_wide.at[hid[h], :])
        target = (grad_gate.at[:, hid[h]], grad_up.at[:, hid[h]], grad_down.at[hid[h], :])
        return pltpu.make_async_copy(source[kind], target[kind], out_sem.at[2 + 3 * h + kind])

    def grad_relay_copy(h, side):
        return remote(
            grad_part.at[across, :, halves[side], hid[h]],
            grad_relay.at[side, :, :, hid[h]],
            [relay_sem.at[h, side, i] for i in range(2)],
            {"rep": beside[side]},
        )

    def grad_copy(h, side):
        return remote(
            grad_part.at[beside[side], :, :, hid[h]],
            grad_in.at[side, :, :, hid[h]],
            [grad_sem.at[h, side, i] for i in range(2)],
            {"rep": beside[side]},
        )

    def make_grads(h):
        for q in range(n_rep):
            columns = slice(q * piece, (q + 1) * piece)
            for kind, (array, by) in enumerate(((0, 1), (0, 2), (1, 0))):
                grad_part[q, kind, :, hid[h]] = dot_first(rows[array, :, columns], act[by, :, hid[h]]).astype(BF)
        for side in range(2):
            grad_relay_copy(h, side).start()

    def pass_grads(h):
        for side in range(2):
            grad_relay_copy(h, side).wait_recv()
            grad_part[beside[side], :, halves[side], hid[h]] = (
                grad_part[beside[side], :, halves[side], hid[h]].astype(F32)
                + grad_relay[side, :, :, hid[h]].astype(F32)
            ).astype(BF)
            grad_copy(h, side).start()

    def add_grads(h):
        for side in range(2):
            grad_copy(h, side).wait_recv()
        for kind in range(3):
            full = (
                grad_part[my_rep, kind, :, hid[h]].astype(F32)
                + grad_in[0, kind, :, hid[h]].astype(F32)
                + grad_in[1, kind, :, hid[h]].astype(F32)
            )
            if kind < 2:
                out_tall[kind, :, hid[h]] = full.astype(BF)
            else:
                out_wide[hid[h], :] = full.T.astype(BF)
            grad_out(h, kind).start()

    with jax.named_scope("entry"):
        pl.semaphore_wait(barrier, n_dp - 1 + 4)
    with jax.named_scope("first_weights"):
        send_weights(0)
    with jax.named_scope("gather_rows"):
        for array in range(2):
            loads[array].wait()
            gather(array)

    with jax.named_scope("issue"):
        exchange(leave.at[0], arrive.at[0], row_sem.at[0])
        exchange(leave.at[1], arrive.at[1], row_sem.at[1])
        for copy in loads[2:]:
            copy.wait()

    def step(name, call, *args):
        with jax.named_scope(name):
            call(*args)

    def grads_and_outputs(h):
        wait_act(h, 0)
        wait_act(h, 1)
        make_grads(h)
        add_outputs(h, 0)
        add_outputs(h, 1)

    step("relay_0", relay_weights, 0)
    step("weights_to_1", send_weights, 1)
    step("tokens", take_rows, 0)
    step("weights_0a", wait_weights, 0, (0, 1))
    step("part_0a", send_part, 0, 0)
    step("cross_0a", cross_part, 0, 0)
    step("relay_1", relay_weights, 1)
    step("weights_to_2", send_weights, 2)
    step("scaled", take_rows, 1)
    step("weights_0b", wait_weights, 0, (2,))
    step("part_0b", send_part, 0, 1)
    step("activate_0a", activate, 0, 0)
    step("cross_0b", cross_part, 0, 1)
    step("relay_2", relay_weights, 2)
    step("weights_1", wait_weights, 1, (0, 1, 2))
    step("part_1a", send_part, 1, 0)
    step("part_1b", send_part, 1, 1)
    step("activate_0b", activate, 0, 1)
    step("act_0a", relay_act, 0, 0)
    step("cross_1a", cross_part, 1, 0)
    step("cross_1b", cross_part, 1, 1)
    step("act_0b", relay_act, 0, 1)
    step("weights_2", wait_weights, 2, (0, 1, 2))
    step("part_2a", send_part, 2, 0)
    step("part_2b", send_part, 2, 1)
    step("activate_1a", activate, 1, 0)
    step("activate_1b", activate, 1, 1)
    step("grads_0", grads_and_outputs, 0)
    step("cross_2a", cross_part, 2, 0)
    step("cross_2b", cross_part, 2, 1)
    step("act_1a", relay_act, 1, 0)
    step("act_1b", relay_act, 1, 1)
    step("activate_2a", activate, 2, 0)
    step("activate_2b", activate, 2, 1)
    step("pass_0", pass_grads, 0)
    step("grads_1", grads_and_outputs, 1)
    step("act_2a", relay_act, 2, 0)
    step("act_2b", relay_act, 2, 1)
    step("wait_2a", wait_act, 2, 0)
    step("outputs_a", add_outputs, 2, 0)
    step("return_a", send_outputs, 0)
    step("wait_2b", wait_act, 2, 1)
    step("outputs_b", add_outputs, 2, 1)
    step("pass_1", pass_grads, 1)
    step("grads_2", make_grads, 2)
    step("return_b", send_outputs, 1)
    step("pass_2", pass_grads, 2)
    step("add_0", add_grads, 0)
    step("add_1", add_grads, 1)
    step("combine_a", combine, 0)
    step("combine_b", combine, 1)
    step("add_2", add_grads, 2)

    with jax.named_scope("drain"):
        for array in range(2):
            wait_exchange(arrive.at[array], row_sem.at[array, 0])
            wait_exchange(back_arrive.at[array], back_sem.at[array, 0])
            row_out(array).wait()
        for h in range(chunks):
            for kind, side in every:
                weight_copy(h, kind, side).wait_send()
                relay_copy(h, kind, side).wait_send()
            for side in range(2):
                grad_relay_copy(h, side).wait_send()
                grad_copy(h, side).wait_send()
            for kind in range(3):
                grad_out(h, kind).wait()

        @pl.when(outer)
        def _():
            for h in range(chunks):
                for group in range(2):
                    for phase in range(2):
                        part_copy(h, group, phase).wait_send()

        @pl.when(inner)
        def _():
            for h in range(chunks):
                for group in range(2):
                    part_copy(h, group, 2).wait_send()
                    for phase in range(3):
                        act_copy(h, group, phase).wait_send()


def finish_kernel(*refs):
    count = (len(refs) - 1) // 2
    copies = [pltpu.make_async_copy(refs[i], refs[count + i], refs[-1].at[i]) for i in range(count)]
    for copy in copies:
        copy.start()
    for copy in copies:
        copy.wait()


def per_device(n_dp, n_ctx, n_rep, tokens, cotangent, routes, gates, replica_of, capacity, w_gate, w_up, w_down):
    count, width = tokens.shape
    buckets = n_dp * n_rep
    slots = CAP * buckets
    lines = CAP * (width // LANES)
    piece = width // n_rep
    hidden = w_gate.shape[2]
    chunks = len(HID_CHUNKS)
    vmem = pl.BlockSpec(memory_space=pltpu.VMEM)
    smem = pl.BlockSpec(memory_space=pltpu.SMEM)
    hbm = pl.BlockSpec(memory_space=pl.ANY)
    outs = (
        jax.ShapeDtypeStruct((count, width), BF),
        jax.ShapeDtypeStruct((count, width), BF),
        jax.ShapeDtypeStruct((piece, hidden), BF),
        jax.ShapeDtypeStruct((piece, hidden), BF),
        jax.ShapeDtypeStruct((hidden, piece), BF),
    )
    results = pl.pallas_call(
        functools.partial(expert_kernel, n_dp, n_ctx, n_rep),
        out_shape=outs,
        in_specs=[smem, smem, vmem, vmem, hbm, hbm, hbm, hbm, hbm],
        out_specs=[hbm] * 5,
        scratch_shapes=[
            pltpu.VMEM((count, width), BF),
            pltpu.VMEM((count, width), BF),
            pltpu.VMEM((slots, count), BF),
            pltpu.VMEM((slots, count), BF),
            pltpu.VMEM((slots, count), BF),
            pltpu.VMEM((2, n_dp, n_rep * lines, LANES), BF),
            pltpu.VMEM((2, n_dp, n_rep * lines, LANES), BF),
            pltpu.VMEM((2, n_dp, n_rep * lines, LANES), BF),
            pltpu.VMEM((2, n_dp, n_rep * lines, LANES), BF),
            pltpu.VMEM((n_rep, piece, hidden), BF),
            pltpu.VMEM((n_rep, piece, hidden), BF),
            pltpu.VMEM((n_rep, hidden, piece), BF),
            pltpu.VMEM((buckets * lines, LANES), F32),
            pltpu.VMEM((2, slots, width), BF),
            pltpu.VMEM((3, slots, hidden), BF),
            pltpu.VMEM((3, 3, slots // 2, hidden), BF),
            pltpu.VMEM((3, slots // 2, hidden), BF),
            pltpu.VMEM((3, slots, hidden), BF),
            pltpu.VMEM((2, slots, width), F32),
            pltpu.VMEM((n_rep, 3, piece, hidden), BF),
            pltpu.VMEM((2, 3, piece // 2, hidden), BF),
            pltpu.VMEM((2, 3, piece, hidden), BF),
            pltpu.VMEM((2, count, width), BF),
            pltpu.VMEM((2, piece, hidden), BF),
            pltpu.VMEM((hidden, piece), BF),
            pltpu.SemaphoreType.DMA((5,)),
            pltpu.SemaphoreType.DMA((2, 2)),
            pltpu.SemaphoreType.DMA((chunks, 3, 2, 4)),
            pltpu.SemaphoreType.DMA((chunks, 2, 3, 2)),
            pltpu.SemaphoreType.DMA((chunks, 2, 3, 2)),
            pltpu.SemaphoreType.DMA((2, 2)),
            pltpu.SemaphoreType.DMA((chunks, 2, 2)),
            pltpu.SemaphoreType.DMA((chunks, 2, 2)),
            pltpu.SemaphoreType.DMA((2 + 3 * chunks,)),
        ],
        compiler_params=pltpu.CompilerParams(
            vmem_limit_bytes=VMEM_BYTES, collective_id=0, has_side_effects=True
        ),
        name="experts",
    )(replica_of, capacity, routes.T, gates.T, tokens, cotangent, w_gate[0], w_up[0], w_down[0])
    layer_out, input_grad, grad_gate, grad_up, grad_down = pl.pallas_call(
        finish_kernel,
        out_shape=outs,
        in_specs=[vmem] * 5,
        out_specs=[hbm] * 5,
        scratch_shapes=[pltpu.SemaphoreType.DMA((5,))],
        name="finish",
    )(*results)
    return layer_out, input_grad, grad_gate[None], grad_up[None], grad_down[None]


def solution(mesh):
    rows = P(("dp", "rep"), "ctx")
    routed = P(("dp", "rep"), None)
    tall = P("dp", ("ctx", "rep"), None)
    wide = P("dp", None, ("ctx", "rep"))
    sizes = dict(mesh.shape)
    return jax.shard_map(
        functools.partial(per_device, sizes["dp"], sizes["ctx"], sizes["rep"]),
        mesh=mesh,
        in_specs=(rows, rows, routed, routed, P(("dp", "rep")), P(), tall, tall, wide),
        out_specs=(rows, rows, tall, tall, wide),
        check_vma=False,
    )
```

```python
import functools

import jax
import jax.numpy as jnp
from jax import lax
from jax.experimental import pallas as pl
from jax.experimental.pallas import tpu as pltpu
from jax.sharding import PartitionSpec as P

MESH = pl.DeviceIdType.MESH
BF = jnp.bfloat16
F32 = jnp.float32
BLK = 16
CAP = 2
LANES = 128
HID_CHUNKS = (384, 256, 128)
VMEM_BYTES = 58 * 1024 * 1024


def dot(left, right):
    return jnp.dot(left, right, preferred_element_type=F32)


def dot_first(left, right):
    return lax.dot_general(left, right, (((0,), (0,)), ((), ())), preferred_element_type=F32)


def dot_last(left, right):
    return lax.dot_general(left, right, (((1,), (1,)), ((), ())), preferred_element_type=F32)


def pack(stage, slot, rows, buckets, tiles):
    for tile in range(tiles):
        stage[pl.ds(slot * tiles + tile, buckets, stride=CAP * tiles), :] = rows[:, tile * LANES : (tile + 1) * LANES]


def unpack(stage, slot, tile, buckets, tiles):
    return stage[pl.ds(slot * tiles + tile, buckets, stride=CAP * tiles), :]


def expert_kernel(
    n_dp,
    n_ctx,
    n_rep,
    replica,
    capacity,
    routes,
    gates,
    tokens,
    cotangent,
    w_gate,
    w_up,
    w_down,
    layer_out,
    input_grad,
    grad_gate,
    grad_up,
    grad_down,
    token_rows,
    cotangent_rows,
    pick,
    pick_hi,
    pick_lo,
    leave,
    arrive,
    back_leave,
    back_arrive,
    all_gate,
    all_up,
    all_down,
    stage,
    rows,
    part,
    inbox,
    cross,
    act,
    total,
    grad_part,
    grad_relay,
    grad_in,
    out_rows,
    out_tall,
    out_wide,
    local_sem,
    row_sem,
    weight_sem,
    part_sem,
    act_sem,
    back_sem,
    relay_sem,
    grad_sem,
    out_sem,
):
    buckets = n_dp * n_rep
    my_dp, my_ctx, my_rep = (lax.axis_index(name) for name in ("dp", "ctx", "rep"))
    right, left = lax.rem(my_rep + 1, n_rep), lax.rem(my_rep + n_rep - 1, n_rep)
    beside = (right, left)
    across = lax.rem(my_rep + 2, n_rep)
    count, width = tokens.shape
    top = routes.shape[0]
    tiles = width // LANES
    piece = width // n_rep
    chunks = len(HID_CHUNKS)
    ends = [sum(HID_CHUNKS[: h + 1]) for h in range(chunks)]
    hid = [slice(end - size, end) for end, size in zip(ends, HID_CHUNKS)]
    share = rows.shape[1] // 2
    inner = jnp.logical_or(my_ctx == 1, my_ctx == 2)
    outer = jnp.logical_not(inner)
    partner = my_ctx + 1 - 2 * lax.rem(my_ctx, 2)
    opposite = n_ctx - 1 - my_ctx
    mine = pl.ds(pl.multiple_of((my_ctx // 2) * share, share), share)
    theirs = pl.ds(pl.multiple_of((1 - my_ctx // 2) * share, share), share)
    groups = (slice(0, 2), slice(2, 3))
    act_groups = (slice(0, 1), slice(1, 3))
    halves = (slice(0, piece // 2), slice(piece // 2, piece))

    def remote(source, target, sem, where):
        return pltpu.make_async_remote_copy(
            src_ref=source,
            dst_ref=target,
            send_sem=sem[0],
            recv_sem=sem[1],
            device_id=where,
            device_id_type=MESH,
        )

    def wait_for(view, sem):
        pltpu.make_async_copy(view, view, sem).wait()

    barrier = pltpu.get_barrier_semaphore()

    def to_others(visit):
        def one(step, carry):
            visit(lax.rem(my_dp + step, n_dp))
            return carry

        lax.fori_loop(1, n_dp, one, 0)

    def greet(where):
        pl.semaphore_signal(barrier, inc=1, device_id=where, device_id_type=MESH)

    with jax.named_scope("greet"):
        to_others(lambda dp: greet({"dp": dp}))
        for rep in beside:
            greet({"rep": rep})
        for ctx in (partner, opposite):
            greet({"ctx": ctx})
        loads = [
            pltpu.make_async_copy(source, target, local_sem.at[kind])
            for kind, (source, target) in enumerate(
                (
                    (tokens, token_rows),
                    (cotangent, cotangent_rows),
                    (w_gate, all_gate.at[my_rep]),
                    (w_up, all_up.at[my_rep]),
                    (w_down, all_down.at[my_rep]),
                )
            )
        ]
        for copy in loads:
            copy.start()

    with jax.named_scope("slots"):
        token = lax.broadcasted_iota(jnp.int32, (1, count), 1)
        serve = jnp.zeros((1, count), jnp.int32)
        for block in range(count // BLK):
            serve = jnp.where(token // BLK == block, replica[block], serve)
        bucket = lax.broadcasted_iota(jnp.int32, (buckets, 1), 0)
        limit = jnp.zeros((buckets, 1), jnp.int32)
        for expert in range(n_dp):
            limit = jnp.where(bucket // n_rep == expert, capacity[expert], limit)
        limit = limit.astype(F32)
        bucket = lax.broadcasted_iota(jnp.int32, (buckets, count), 0)
        earlier = jnp.where(
            lax.broadcasted_iota(jnp.int32, (count, count), 0) < lax.broadcasted_iota(jnp.int32, (count, count), 1),
            1.0,
            0.0,
        ).astype(BF)
        seen = jnp.zeros((buckets, 1), F32)
        kept = [jnp.zeros((buckets, count), F32) for _ in range(CAP)]
        weight = [jnp.zeros((buckets, count), F32) for _ in range(CAP)]
        for k in range(top):
            ones = jnp.where(bucket == routes[k : k + 1, :] * n_rep + serve, 1.0, 0.0)
            slot_of = dot(ones.astype(BF), earlier) + seen
            seen = seen + jnp.sum(ones, axis=1, keepdims=True)
            gate = gates[k : k + 1, :]
            for slot in range(CAP):
                here = jnp.where((slot_of == float(slot)) & (limit > float(slot)), ones, 0.0)
                kept[slot] = kept[slot] + here
                weight[slot] = weight[slot] + here * gate
        for slot in range(CAP):
            taken = slice(slot * buckets, (slot + 1) * buckets)
            high = weight[slot].astype(BF)
            pick[taken, :] = kept[slot].astype(BF)
            pick_hi[taken, :] = high
            pick_lo[taken, :] = (weight[slot] - high.astype(F32)).astype(BF)

    def gather(array):
        for slot in range(CAP):
            taken = slice(slot * buckets, (slot + 1) * buckets)
            if array == 0:
                picked = dot(pick[taken, :], token_rows[...])
            else:
                picked = dot(pick_hi[taken, :], cotangent_rows[...]) + dot(pick_lo[taken, :], cotangent_rows[...])
            pack(stage, slot, picked, buckets, tiles)
        leave[array] = stage[...].astype(BF).reshape(leave.shape[1:])

    weights = (
        (lambda h: w_gate.at[:, hid[h]], lambda q, h: all_gate.at[q, :, hid[h]]),
        (lambda h: w_up.at[:, hid[h]], lambda q, h: all_up.at[q, :, hid[h]]),
        (lambda h: w_down.at[hid[h], :], lambda q, h: all_down.at[q, hid[h], :]),
    )
    half_views = (
        lambda q, h, side: all_gate.at[q, halves[side], hid[h]],
        lambda q, h, side: all_up.at[q, halves[side], hid[h]],
        lambda q, h, side: all_down.at[
            q, slice(hid[h].start + side * HID_CHUNKS[h] // 2, hid[h].start + (side + 1) * HID_CHUNKS[h] // 2), :
        ],
    )

    def weight_copy(h, kind, side):
        source, target = weights[kind]
        return remote(
            source(h), target(my_rep, h), [weight_sem.at[h, kind, side, i] for i in range(2)], {"rep": beside[side]}
        )

    def relay_copy(h, kind, side):
        block = half_views[kind](beside[1 - side], h, side)
        return remote(block, block, [weight_sem.at[h, kind, side, 2 + i] for i in range(2)], {"rep": beside[side]})

    every = [(kind, side) for kind in range(3) for side in range(2)]

    def send_weights(h):
        for kind, side in every:
            weight_copy(h, kind, side).start()

    def relay_weights(h):
        for kind, side in every:
            weight_copy(h, kind, side).wait_recv()
            relay_copy(h, kind, side).start()

    def wait_weights(h, kinds):
        for kind in kinds:
            for side in range(2):
                relay_copy(h, kind, side).wait_recv()

    def exchange(source, target, sem):
        def send(dp):
            remote(source.at[dp], target.at[my_dp], (sem.at[0], sem.at[1]), {"dp": dp}).start()

        to_others(send)
        target[my_dp] = source[my_dp]

    def wait_exchange(target, sem):
        wait_for(target.at[pl.ds(0, n_dp - 1)], sem)

    def take_rows(array):
        wait_exchange(arrive.at[array], row_sem.at[array, 1])
        stage[...] = arrive[array].astype(F32).reshape(stage.shape)
        for slot in range(CAP):
            for tile in range(tiles):
                rows[array, slot * buckets : (slot + 1) * buckets, tile * LANES : (tile + 1) * LANES] = unpack(
                    stage, slot, tile, buckets, tiles
                ).astype(BF)

    def part_copy(h, group, phase):
        source = (part.at[groups[group], theirs, hid[h]], part.at[groups[group], mine, hid[h]], cross.at[groups[group], :, hid[h]])
        return remote(
            source[phase],
            inbox.at[phase, groups[group], :, hid[h]],
            [part_sem.at[h, group, phase, i] for i in range(2)],
            {"ctx": opposite if phase == 2 else partner},
        )

    def send_part(h, group):
        if group == 0:
            for kind, full in enumerate((all_gate, all_up)):
                part[kind, :, hid[h]] = dot(rows[0], full[:, :, hid[h]].reshape(width, HID_CHUNKS[h])).astype(BF)
        else:
            part[2, :, hid[h]] = sum(
                dot_last(rows[1, :, q * piece : (q + 1) * piece], all_down[q, hid[h], :]) for q in range(n_rep)
            ).astype(BF)

        @pl.when(outer)
        def _():
            part_copy(h, group, 0).start()
            part_copy(h, group, 1).start()

    def cross_part(h, group):
        @pl.when(inner)
        def _():
            part_copy(h, group, 0).wait_recv()
            for kind in range(3)[groups[group]]:
                cross[kind, :, hid[h]] = (
                    part[kind, theirs, hid[h]].astype(F32) + inbox[0, kind, :, hid[h]].astype(F32)
                ).astype(BF)
            part_copy(h, group, 2).start()

    def summed(h, kind):
        return (
            part[kind, mine, hid[h]].astype(F32)
            + inbox[1, kind, :, hid[h]].astype(F32)
            + inbox[2, kind, :, hid[h]].astype(F32)
        )

    def act_copy(h, group, phase):
        block = act.at[act_groups[group], theirs if phase == 2 else mine, hid[h]]
        return remote(
            block,
            block,
            [act_sem.at[h, group, phase, i] for i in range(2)],
            {"ctx": opposite if phase == 0 else partner},
        )

    def activate(h, group):
        @pl.when(inner)
        def _():
            part_copy(h, group, 1).wait_recv()
            part_copy(h, group, 2).wait_recv()
            pre_gate, pre_up = summed(h, 0), summed(h, 1)
            sigmoid = jax.nn.sigmoid(pre_gate)
            swish = pre_gate * sigmoid
            if group == 0:
                act[0, mine, hid[h]] = (swish * pre_up).astype(BF)
            else:
                grad = summed(h, 2)
                act[1, mine, hid[h]] = (grad * pre_up * sigmoid * (1.0 + pre_gate * (1.0 - sigmoid))).astype(BF)
                act[2, mine, hid[h]] = (grad * swish).astype(BF)
            act_copy(h, group, 0).start()
            act_copy(h, group, 1).start()

    def relay_act(h, group):
        @pl.when(inner)
        def _():
            act_copy(h, group, 0).wait_recv()
            act_copy(h, group, 2).start()

    def wait_act(h, group):
        @pl.when(outer)
        def _():
            act_copy(h, group, 1).wait_recv()
            act_copy(h, group, 2).wait_recv()

    def add_outputs(h, array):
        for q in range(n_rep):
            columns = slice(q * piece, (q + 1) * piece)
            if array == 0:
                term = dot(act[0, :, hid[h]], all_down[q, hid[h], :])
            else:
                term = dot_last(act[1, :, hid[h]], all_gate[q, :, hid[h]]) + dot_last(
                    act[2, :, hid[h]], all_up[q, :, hid[h]]
                )
            total[array, :, columns] = term + total[array, :, columns] if h else term

    def send_outputs(array):
        for slot in range(CAP):
            pack(stage, slot, total[array, slot * buckets : (slot + 1) * buckets, :], buckets, tiles)
        back_leave[array] = stage[...].astype(BF).reshape(back_leave.shape[1:])
        exchange(back_leave.at[array], back_arrive.at[array], back_sem.at[array])

    def combine(array):
        wait_exchange(back_arrive.at[array], back_sem.at[array, 1])
        stage[...] = back_arrive[array].astype(F32).reshape(stage.shape)
        for tile in range(tiles):
            block = jnp.concatenate(
                [unpack(stage, slot, tile, buckets, tiles) for slot in range(CAP)], axis=0
            ).astype(BF)
            columns = slice(tile * LANES, (tile + 1) * LANES)
            if array == 0:
                out_rows[0, :, columns] = (dot_first(pick_hi[...], block) + dot_first(pick_lo[...], block)).astype(BF)
            else:
                out_rows[1, :, columns] = dot_first(pick[...], block).astype(BF)
        row_out(array).start()

    def row_out(array):
        return pltpu.make_async_copy(out_rows.at[array], (layer_out, input_grad)[array], out_sem.at[array])

    def grad_out(h, kind):
        source = (out_tall.at[0, :, hid[h]], out_tall.at[1, :, hid[h]], out_wide.at[hid[h], :])
        target = (grad_gate.at[:, hid[h]], grad_up.at[:, hid[h]], grad_down.at[hid[h], :])
        return pltpu.make_async_copy(source[kind], target[kind], out_sem.at[2 + 3 * h + kind])

    def grad_relay_copy(h, side):
        return remote(
            grad_part.at[across, :, halves[side], hid[h]],
            grad_relay.at[side, :, :, hid[h]],
            [relay_sem.at[h, side, i] for i in range(2)],
            {"rep": beside[side]},
        )

    def grad_copy(h, side):
        return remote(
            grad_part.at[beside[side], :, :, hid[h]],
            grad_in.at[side, :, :, hid[h]],
            [grad_sem.at[h, side, i] for i in range(2)],
            {"rep": beside[side]},
        )

    def make_grads(h):
        for q in range(n_rep):
            columns = slice(q * piece, (q + 1) * piece)
            for kind, (array, by) in enumerate(((0, 1), (0, 2), (1, 0))):
                grad_part[q, kind, :, hid[h]] = dot_first(rows[array, :, columns], act[by, :, hid[h]]).astype(BF)
        for side in range(2):
            grad_relay_copy(h, side).start()

    def pass_grads(h):
        for side in range(2):
            grad_relay_copy(h, side).wait_recv()
            grad_part[beside[side], :, halves[side], hid[h]] = (
                grad_part[beside[side], :, halves[side], hid[h]].astype(F32)
                + grad_relay[side, :, :, hid[h]].astype(F32)
            ).astype(BF)
            grad_copy(h, side).start()

    def add_grads(h):
        for side in range(2):
            grad_copy(h, side).wait_recv()
        for kind in range(3):
            full = (
                grad_part[my_rep, kind, :, hid[h]].astype(F32)
                + grad_in[0, kind, :, hid[h]].astype(F32)
                + grad_in[1, kind, :, hid[h]].astype(F32)
            )
            if kind < 2:
                out_tall[kind, :, hid[h]] = full.astype(BF)
            else:
                out_wide[hid[h], :] = full.T.astype(BF)
            grad_out(h, kind).start()

    with jax.named_scope("entry"):
        pl.semaphore_wait(barrier, n_dp - 1 + 4)
    with jax.named_scope("first_weights"):
        send_weights(0)
    with jax.named_scope("gather_rows"):
        for array in range(2):
            loads[array].wait()
            gather(array)

    with jax.named_scope("issue"):
        exchange(leave.at[0], arrive.at[0], row_sem.at[0])
        exchange(leave.at[1], arrive.at[1], row_sem.at[1])
        for copy in loads[2:]:
            copy.wait()

    def step(name, call, *args):
        with jax.named_scope(name):
            call(*args)

    def grads_and_outputs(h):
        wait_act(h, 0)
        wait_act(h, 1)
        make_grads(h)
        add_outputs(h, 0)
        add_outputs(h, 1)

    step("relay_0", relay_weights, 0)
    step("weights_to_1", send_weights, 1)
    step("tokens", take_rows, 0)
    step("weights_0a", wait_weights, 0, (0, 1))
    step("part_0a", send_part, 0, 0)
    step("cross_0a", cross_part, 0, 0)
    step("relay_1", relay_weights, 1)
    step("weights_to_2", send_weights, 2)
    step("scaled", take_rows, 1)
    step("weights_0b", wait_weights, 0, (2,))
    step("part_0b", send_part, 0, 1)
    step("activate_0a", activate, 0, 0)
    step("cross_0b", cross_part, 0, 1)
    step("relay_2", relay_weights, 2)
    step("weights_1", wait_weights, 1, (0, 1, 2))
    step("part_1a", send_part, 1, 0)
    step("part_1b", send_part, 1, 1)
    step("activate_0b", activate, 0, 1)
    step("act_0a", relay_act, 0, 0)
    step("cross_1a", cross_part, 1, 0)
    step("cross_1b", cross_part, 1, 1)
    step("act_0b", relay_act, 0, 1)
    step("weights_2", wait_weights, 2, (0, 1, 2))
    step("part_2a", send_part, 2, 0)
    step("part_2b", send_part, 2, 1)
    step("activate_1a", activate, 1, 0)
    step("activate_1b", activate, 1, 1)
    step("grads_0", grads_and_outputs, 0)
    step("cross_2a", cross_part, 2, 0)
    step("cross_2b", cross_part, 2, 1)
    step("act_1a", relay_act, 1, 0)
    step("act_1b", relay_act, 1, 1)
    step("activate_2a", activate, 2, 0)
    step("activate_2b", activate, 2, 1)
    step("pass_0", pass_grads, 0)
    step("grads_1", grads_and_outputs, 1)
    step("act_2a", relay_act, 2, 0)
    step("act_2b", relay_act, 2, 1)
    step("wait_2a", wait_act, 2, 0)
    step("wait_2b", wait_act, 2, 1)
    step("grads_2", make_grads, 2)
    step("outputs_a", add_outputs, 2, 0)
    step("return_a", send_outputs, 0)
    step("pass_1", pass_grads, 1)
    step("outputs_b", add_outputs, 2, 1)
    step("return_b", send_outputs, 1)
    step("pass_2", pass_grads, 2)
    step("add_0", add_grads, 0)
    step("add_1", add_grads, 1)
    step("combine_a", combine, 0)
    step("combine_b", combine, 1)
    step("add_2", add_grads, 2)

    with jax.named_scope("drain"):
        for array in range(2):
            wait_exchange(arrive.at[array], row_sem.at[array, 0])
            wait_exchange(back_arrive.at[array], back_sem.at[array, 0])
            row_out(array).wait()
        for h in range(chunks):
            for kind, side in every:
                weight_copy(h, kind, side).wait_send()
                relay_copy(h, kind, side).wait_send()
            for side in range(2):
                grad_relay_copy(h, side).wait_send()
                grad_copy(h, side).wait_send()
            for kind in range(3):
                grad_out(h, kind).wait()

        @pl.when(outer)
        def _():
            for h in range(chunks):
                for group in range(2):
                    for phase in range(2):
                        part_copy(h, group, phase).wait_send()

        @pl.when(inner)
        def _():
            for h in range(chunks):
                for group in range(2):
                    part_copy(h, group, 2).wait_send()
                    for phase in range(3):
                        act_copy(h, group, phase).wait_send()


def finish_kernel(*refs):
    count = (len(refs) - 1) // 2
    copies = [pltpu.make_async_copy(refs[i], refs[count + i], refs[-1].at[i]) for i in range(count)]
    for copy in copies:
        copy.start()
    for copy in copies:
        copy.wait()


def per_device(n_dp, n_ctx, n_rep, tokens, cotangent, routes, gates, replica_of, capacity, w_gate, w_up, w_down):
    count, width = tokens.shape
    buckets = n_dp * n_rep
    slots = CAP * buckets
    lines = CAP * (width // LANES)
    piece = width // n_rep
    hidden = w_gate.shape[2]
    chunks = len(HID_CHUNKS)
    vmem = pl.BlockSpec(memory_space=pltpu.VMEM)
    smem = pl.BlockSpec(memory_space=pltpu.SMEM)
    hbm = pl.BlockSpec(memory_space=pl.ANY)
    outs = (
        jax.ShapeDtypeStruct((count, width), BF),
        jax.ShapeDtypeStruct((count, width), BF),
        jax.ShapeDtypeStruct((piece, hidden), BF),
        jax.ShapeDtypeStruct((piece, hidden), BF),
        jax.ShapeDtypeStruct((hidden, piece), BF),
    )
    results = pl.pallas_call(
        functools.partial(expert_kernel, n_dp, n_ctx, n_rep),
        out_shape=outs,
        in_specs=[smem, smem, vmem, vmem, hbm, hbm, hbm, hbm, hbm],
        out_specs=[hbm] * 5,
        scratch_shapes=[
            pltpu.VMEM((count, width), BF),
            pltpu.VMEM((count, width), BF),
            pltpu.VMEM((slots, count), BF),
            pltpu.VMEM((slots, count), BF),
            pltpu.VMEM((slots, count), BF),
            pltpu.VMEM((2, n_dp, n_rep * lines, LANES), BF),
            pltpu.VMEM((2, n_dp, n_rep * lines, LANES), BF),
            pltpu.VMEM((2, n_dp, n_rep * lines, LANES), BF),
            pltpu.VMEM((2, n_dp, n_rep * lines, LANES), BF),
            pltpu.VMEM((n_rep, piece, hidden), BF),
            pltpu.VMEM((n_rep, piece, hidden), BF),
            pltpu.VMEM((n_rep, hidden, piece), BF),
            pltpu.VMEM((buckets * lines, LANES), F32),
            pltpu.VMEM((2, slots, width), BF),
            pltpu.VMEM((3, slots, hidden), BF),
            pltpu.VMEM((3, 3, slots // 2, hidden), BF),
            pltpu.VMEM((3, slots // 2, hidden), BF),
            pltpu.VMEM((3, slots, hidden), BF),
            pltpu.VMEM((2, slots, width), F32),
            pltpu.VMEM((n_rep, 3, piece, hidden), BF),
            pltpu.VMEM((2, 3, piece // 2, hidden), BF),
            pltpu.VMEM((2, 3, piece, hidden), BF),
            pltpu.VMEM((2, count, width), BF),
            pltpu.VMEM((2, piece, hidden), BF),
            pltpu.VMEM((hidden, piece), BF),
            pltpu.SemaphoreType.DMA((5,)),
            pltpu.SemaphoreType.DMA((2, 2)),
            pltpu.SemaphoreType.DMA((chunks, 3, 2, 4)),
            pltpu.SemaphoreType.DMA((chunks, 2, 3, 2)),
            pltpu.SemaphoreType.DMA((chunks, 2, 3, 2)),
            pltpu.SemaphoreType.DMA((2, 2)),
            pltpu.SemaphoreType.DMA((chunks, 2, 2)),
            pltpu.SemaphoreType.DMA((chunks, 2, 2)),
            pltpu.SemaphoreType.DMA((2 + 3 * chunks,)),
        ],
        compiler_params=pltpu.CompilerParams(
            vmem_limit_bytes=VMEM_BYTES, collective_id=0, has_side_effects=True
        ),
        name="experts",
    )(replica_of, capacity, routes.T, gates.T, tokens, cotangent, w_gate[0], w_up[0], w_down[0])
    layer_out, input_grad, grad_gate, grad_up, grad_down = pl.pallas_call(
        finish_kernel,
        out_shape=outs,
        in_specs=[vmem] * 5,
        out_specs=[hbm] * 5,
        scratch_shapes=[pltpu.SemaphoreType.DMA((5,))],
        name="finish",
    )(*results)
    return layer_out, input_grad, grad_gate[None], grad_up[None], grad_down[None]


def solution(mesh):
    rows = P(("dp", "rep"), "ctx")
    routed = P(("dp", "rep"), None)
    tall = P("dp", ("ctx", "rep"), None)
    wide = P("dp", None, ("ctx", "rep"))
    sizes = dict(mesh.shape)
    return jax.shard_map(
        functools.partial(per_device, sizes["dp"], sizes["ctx"], sizes["rep"]),
        mesh=mesh,
        in_specs=(rows, rows, routed, routed, P(("dp", "rep")), P(), tall, tall, wide),
        out_specs=(rows, rows, tall, tall, wide),
        check_vma=False,
    )
```
